512 devices in a mesh: prompt: 16 (over z_hi, y), tp: 32 (over x, z_lo, core).
Axes of the slice: x: 4, y: 4, z: 16 (z_hi: 4, z_lo: 4; z = z_hi * 4 + z_lo), core: 2. Of those that a mesh axis runs over, the one named last changes fastest.
Arguments:
- prompt_keys: bfloat16 [16, 8, 8192, 128], P('prompt', None, 'tp'), may hold values from -13 to 13
- prompt_values: bfloat16 [16, 8, 8192, 128], P('prompt', None, 'tp'), may hold values from -24 to 24
- queries: bfloat16 [16, 3, 64, 16384], P('prompt', None, None, 'tp'), may hold values from -80 to 80
- sample_step_keys: bfloat16 [16, 3, 64, 8, 128], P('prompt', None, 'tp'), may hold values from -9 to 9
- suffix_values: bfloat16 [16, 3, 64, 8, 128], P('prompt', None, 'tp'), may hold values from -24 to 24
- suffix_lengths: int32 [16, 64], P('prompt'), may hold values from 1 to 3, as said below
- assignment: int32 [16], replicated, may hold values from 0 to 15, each once
Outputs:
- attended: bfloat16 [16, 3, 64, 16384], P('prompt', None, None, 'tp')
The draws below stay inside these ranges and needn't reach their ends.
Inputs may be any that keep to these rules, and one draw needn't show every extreme that they name: `suffix_lengths`: in every rollout group some sample generates 3 tokens and some sample generates 1.
All inputs are finite; a program needn't handle non-finite values.
Results may differ from the reference program's by a relative error of at most 0.0038.
Values may be sent and summed in bfloat16 or wider, within the bound.
No kernel may reach another device: no remote copies, remote signals or barrier semaphores. Data moves between devices by JAX's collectives and lax.ppermute only.
A program may use at most 64 MiB of HBM per device.

```python
import jax
import jax.numpy as jnp
from jax import lax

Q_HEADS = 128
KV_HEADS = 8
HD = 128
PREFIX = 8192
SAMPLES = 64
STEPS = 3
PROMPTS = 16


def draw_prompt_keys(key, part):
    key = jax.random.fold_in(key, 1)
    base = jnp.clip(jax.random.normal(key, (PROMPTS, KV_HEADS, PREFIX, HD), jnp.float32), -6.0, 6.0)
    return base.astype(jnp.bfloat16)


def draw_queries(key, part):
    key = jax.random.fold_in(key, 2)
    shape = (PROMPTS, STEPS, SAMPLES, Q_HEADS * HD)
    base = jnp.clip(jax.random.normal(key, shape, jnp.float32) * 2.0, -12.0, 12.0)
    return base.astype(jnp.bfloat16)


def draw_suffix_lengths(key, part):
    key = jax.random.fold_in(key, 3)
    lengths = jax.random.randint(key, (PROMPTS, SAMPLES), 1, STEPS + 1, jnp.int32)
    sample = lax.broadcasted_iota(jnp.int32, (PROMPTS, SAMPLES), 1)
    lengths = jnp.where(sample == 0, STEPS, jnp.where(sample == 1, 1, lengths))
    return lengths.astype(jnp.int32)


def block_levels(own_key, dims, pieces, smallest, top_value):
    loudness, own = 1.0, jax.random.fold_in(own_key, 6)
    for dim, parts in pieces:
        heights = jnp.exp(jax.random.uniform(jax.random.fold_in(own, dim), (parts,), jnp.float32, smallest / len(pieces), top_value / len(pieces)))
        loudness = loudness * jnp.repeat(heights, dims[dim] // parts).reshape([-1 if axis == dim else 1 for axis in range(len(dims))])
    return loudness


def bell_draw(key, shape, width, bound, split=(), kind=jnp.bfloat16):
    array = jax.random.normal(key, shape, jnp.float32) * width
    if len(split) > 0:
        array = block_levels(key, shape, split, -0.22, 0.18) * array
    return jnp.clip(array, min=-bound, max=bound).astype(kind)


def setup_inputs(seed: int = 0) -> dict:
    keys = jax.random.split(jax.random.key(seed), 8)
    prompt_keys = draw_prompt_keys(jax.random.fold_in(keys[7], 71), 0)
    prompt_values = bell_draw(keys[1], (PROMPTS, KV_HEADS, PREFIX, HD), 4.0, 24.0, ((0, 16), (2, 32)))
    queries = draw_queries(jax.random.fold_in(keys[7], 71), 0)
    sample_step_keys = bell_draw(keys[3], (PROMPTS, STEPS, SAMPLES, KV_HEADS, HD), 1.5, 9.0, ((0, 16), (2, 32)))
    suffix_values = bell_draw(keys[4], (PROMPTS, STEPS, SAMPLES, KV_HEADS, HD), 4.0, 24.0, ((0, 16), (2, 32)))
    suffix_lengths = draw_suffix_lengths(jax.random.fold_in(keys[7], 71), 0)
    assignment = jax.random.permutation(keys[6], PROMPTS).astype(jnp.int32)
    return dict(prompt_keys=prompt_keys, prompt_values=prompt_values, queries=queries, sample_step_keys=sample_step_keys, suffix_values=suffix_values, suffix_lengths=suffix_lengths, assignment=assignment)


def head_attend_fn(query_head, key_rows, value_rows, suffix_key_rows, suffix_value_rows, live_samples):
    score_scale = HD ** -0.5
    rows = query_head.reshape(-1, HD)
    prefix = jnp.dot(rows, key_rows.T, preferred_element_type=jnp.float32) * score_scale
    suffix_tokens = jnp.einsum("evyc,wvc->evyw", query_head.astype(jnp.float32), suffix_key_rows.astype(jnp.float32)) * score_scale
    step_now = lax.broadcasted_iota(jnp.int32, (STEPS, 1, 1, STEPS), 0)
    step_key = lax.broadcasted_iota(jnp.int32, (STEPS, 1, 1, STEPS), 3)
    causal = step_key <= step_now
    suffix_tokens = jnp.where(causal, suffix_tokens, -jnp.inf)
    top = jnp.maximum(jnp.max(prefix, axis=-1), jnp.max(suffix_tokens, axis=-1).reshape(-1))
    weight_pre = jnp.exp(prefix - top[:, None])
    weight_suf = jnp.where(causal, jnp.exp(suffix_tokens - top.reshape(suffix_tokens.shape[:3])[..., None]), 0.0)
    total = jnp.sum(weight_pre, axis=-1) + jnp.sum(weight_suf, axis=-1).reshape(-1)
    rounded_suf = lax.optimization_barrier(weight_suf.astype(jnp.bfloat16)).astype(jnp.float32)
    numer = jnp.dot(weight_pre.astype(jnp.bfloat16), value_rows, preferred_element_type=jnp.float32)
    numer = numer + jnp.einsum("siht,tid->sihd", rounded_suf, suffix_value_rows.astype(jnp.float32)).reshape(-1, HD)
    result = (numer / total[:, None]).reshape(query_head.shape)
    result = jnp.where(live_samples[:, :, None, None], result, 0.0)
    return result.astype(jnp.bfloat16)


def reference(prompt_keys, prompt_values, queries, sample_step_keys, suffix_values, suffix_lengths, assignment):
    per_kv = Q_HEADS // KV_HEADS

    def one_group(sample_group):
        served = jnp.take(assignment, sample_group)
        keys_all = jnp.take(prompt_keys, served, axis=0)
        value_rows_every = jnp.take(prompt_values, served, axis=0)
        grouped = jnp.take(queries, sample_group, axis=0).reshape(STEPS, SAMPLES, KV_HEADS, per_kv, HD)
        suffix_keys_every = jnp.take(sample_step_keys, sample_group, axis=0)
        svalues_all = jnp.take(suffix_values, sample_group, axis=0)
        lengths = jnp.take(suffix_lengths, sample_group, axis=0)
        live_samples = jnp.arange(STEPS, dtype=jnp.int32)[:, None] < lengths[None, :]

        def one_head(head_index):
            return head_attend_fn(jnp.take(grouped, head_index, axis=2), jnp.take(keys_all, head_index, axis=0),
                               jnp.take(value_rows_every, head_index, axis=0), jnp.take(suffix_keys_every, head_index, axis=2),
                               jnp.take(svalues_all, head_index, axis=2), live_samples)

        heads = lax.map(one_head, jnp.arange(KV_HEADS, dtype=jnp.int32))
        return jnp.moveaxis(heads, 0, 2).reshape(STEPS, SAMPLES, Q_HEADS * HD)

    return lax.map(one_group, jnp.arange(PROMPTS, dtype=jnp.int32))
```

```python
import functools
import math

import jax
import jax.numpy as jnp
from jax import lax
from jax.experimental import pallas as pl
from jax.experimental.pallas import tpu as pltpu
from jax.sharding import PartitionSpec as P

F32 = jnp.float32
BF16 = jnp.bfloat16
NEG = -1e30
VMEM = pl.BlockSpec(memory_space=pltpu.VMEM)

STEPS, SAMPLES, HD = 3, 64, 128
HEADS = 4
TOKENS = STEPS * SAMPLES
ROWS = HEADS * TOKENS
BLOCK = 256
SUF = 16
PART = 2 * BLOCK + SUF
PIECES = 16
PIECE = ROWS // PIECES
EXTRA = 16
SCALE2 = HD ** (-0.5) * math.log2(math.e)
TILE = 256


def dot_t(a, b):
    return lax.dot_general(a, b, (((1,), (1,)), ((), ())), preferred_element_type=F32)


def dot(a, b):
    return lax.dot_general(a, b, (((1,), (0,)), ((), ())), preferred_element_type=F32)


def split3(x):
    hi = x.astype(BF16)
    rest = x - hi.astype(F32)
    mid = rest.astype(BF16)
    low = (rest - mid.astype(F32)).astype(BF16)
    return hi, mid, low


def attend_tile(q, blocks, m, l, acc):
    scores = [dot_t(q, k[...]) for k, _ in blocks]
    top = functools.reduce(jnp.maximum, scores)
    m_new = jnp.maximum(m, jnp.max(top, axis=-1, keepdims=True) * SCALE2)
    fade = jnp.exp2(m - m_new)
    l = l * fade
    acc = acc * fade
    for s, (_, v) in zip(scores, blocks):
        w = jnp.exp2(s * SCALE2 - m_new)
        l = l + jnp.sum(w, axis=-1, keepdims=True)
        acc = acc + dot(w.astype(BF16), v[...])
    return m_new, l, acc


def views(ref):
    return [
        (ref.at[i, pl.ds(0, BLOCK)], ref.at[i, pl.ds(BLOCK, BLOCK)]) for i in range(ref.shape[0])
    ]


def first_kernel(q_ref, a, b, c, d, m_ref, l_ref, acc_ref):
    def body(r, carry):
        at = pl.ds(pl.multiple_of(r * TILE, TILE), TILE)
        q = q_ref[at]
        m = jnp.full((TILE, 1), NEG, F32)
        l = jnp.zeros((TILE, 1), F32)
        acc = jnp.zeros((TILE, HD), F32)
        for ref in (a, b, c, d):
            m, l, acc = attend_tile(q, views(ref), m, l, acc)
        m_ref[at] = jnp.broadcast_to(m, (TILE, HD))
        l_ref[at] = jnp.broadcast_to(l, (TILE, HD))
        acc_ref[at] = acc
        return carry

    lax.fori_loop(0, ROWS // TILE, body, 0)


def second_kernel(q_ref, a, b, c, d, m_ref, l_ref, acc_ref, out_ref, o_sc, lse_sc):
    def body(r, carry):
        at = pl.ds(pl.multiple_of(r * TILE, TILE), TILE)
        q = q_ref[at]
        m, l, acc = m_ref[at][:, :1], l_ref[at][:, :1], acc_ref[at]
        for ref in (a, b, c, d):
            m, l, acc = attend_tile(q, views(ref), m, l, acc)
        o_sc[at] = (acc / l).astype(BF16)
        hi, mid, low = split3(m + jnp.log2(l))
        lane = lax.broadcasted_iota(jnp.int32, (TILE, HD), 1)
        zero = jnp.zeros((TILE, HD), BF16)
        lse_sc[at] = jnp.where(
            lane == 0, hi, jnp.where(lane == 1, mid, jnp.where(lane == 2, low, zero))
        )
        return carry

    lax.fori_loop(0, ROWS // TILE, body, 0)
    row = lax.broadcasted_iota(jnp.int32, (PIECE, HD), 0)
    lane = lax.broadcasted_iota(jnp.int32, (PIECE, HD), 1)
    eye = (row == lane).astype(BF16)
    for p in range(PIECES):
        out_ref[p, pl.ds(0, PIECE)] = o_sc[pl.ds(p * PIECE, PIECE)]
        turned = lax.dot_general(
            lse_sc[pl.ds(p * PIECE, PIECE)],
            eye,
            (((0,), (0,)), ((), ())),
            preferred_element_type=F32,
        )
        out_ref[p, pl.ds(PIECE, EXTRA)] = turned[:EXTRA].astype(BF16)


def suffix_kernel(q_ref, k_ref, v_ref, step_ref, sample_ref, o_ref, lse_ref):
    row = lax.broadcasted_iota(jnp.int32, (TOKENS, TOKENS), 0)
    keep = (sample_ref[...] == row % SAMPLES) & (step_ref[...] <= row // SAMPLES)
    for j in range(HEADS):
        at = pl.ds(j * TOKENS, TOKENS)
        t = jnp.where(keep, dot_t(q_ref[at], k_ref[...]) * SCALE2, NEG)
        m = jnp.max(t, axis=-1, keepdims=True)
        w = jnp.where(keep, jnp.exp2(t - m), 0.0)
        l = jnp.sum(w, axis=-1, keepdims=True)
        o_ref[at] = dot(w.astype(BF16), v_ref[...]) / l
        lse_ref[at] = jnp.broadcast_to(m + jnp.log2(l), (TOKENS, HD))


def merge_kernel(r_ref, o_ref, lse_ref, live_ref, out_ref):
    row = lax.broadcasted_iota(jnp.int32, (PIECE, HD), 0)
    lane = lax.broadcasted_iota(jnp.int32, (PIECE, HD), 1)
    eye = (row == lane).astype(BF16)
    per_head = PIECES // HEADS
    for p in range(PIECES):
        parts = dot_t(eye, r_ref[p, pl.ds(PIECE, EXTRA)])
        lse_p = parts[:, 0:1] + parts[:, 1:2] + parts[:, 2:3]
        at = pl.ds(p * PIECE, PIECE)
        lse_s = lse_ref[at]
        top = jnp.maximum(lse_p, lse_s)
        w_p = jnp.exp2(lse_p - top)
        w_s = jnp.exp2(lse_s - top)
        o_p = r_ref[p, pl.ds(0, PIECE)].astype(F32)
        merged = (w_p * o_p + w_s * o_ref[at]) / (w_p + w_s)
        tok = pl.ds((p % per_head) * PIECE, PIECE)
        merged = jnp.where(live_ref[tok] > 0, merged, 0.0)
        out_ref[tok, pl.ds((p // per_head) * HD, HD)] = merged.astype(BF16)


def call(kernel, outs, args, scratch=(), flops=0, exps=0):
    moved = sum(math.prod(a.shape) * a.dtype.itemsize for a in (*args, *outs))
    many = len(outs) > 1
    return pl.pallas_call(
        kernel,
        out_shape=tuple(outs) if many else outs[0],
        in_specs=[VMEM] * len(args),
        out_specs=(VMEM,) * len(outs) if many else VMEM,
        scratch_shapes=list(scratch),
        compiler_params=pltpu.CompilerParams(vmem_limit_bytes=40 * 2**20),
        cost_estimate=pl.CostEstimate(flops=flops, bytes_accessed=moved, transcendentals=exps),
    )(*args)


def sds(*shape, dtype=F32):
    return jax.ShapeDtypeStruct(shape, dtype)


def local(
    prompt_keys, prompt_values, queries, sample_step_keys, suffix_values, suffix_lengths, assignment
):
    tp = lax.axis_index("tp")
    x, side = tp // 8, (tp // 4) % 2
    keys, values = prompt_keys[0], prompt_values[0]

    def by_head(a):
        return jnp.transpose(a[0], (2, 0, 1, 3)).reshape(8, STEPS * 2, HD)

    fresh = jnp.concatenate(
        [by_head(sample_step_keys), by_head(suffix_values), jnp.zeros((8, 4, HD), BF16)], axis=1
    )

    def payload(to):
        own, other = 2 * to + side, 2 * to + 1 - side
        parts = [
            lax.dynamic_index_in_dim(a, h, 0, keepdims=False)
            for h in (own, other)
            for a in (keys, values, fresh)
        ]
        return jnp.concatenate(parts, axis=0).reshape(2, PART, HD)

    def shift_x(k):
        return [(t, (t + 8 * k) % 32) for t in range(32)]

    def swap(bit):
        return [(t, t ^ bit) for t in range(32)]

    got = [payload(x)] + [
        lax.ppermute(payload((x + k) % 4), "tp", shift_x(k)) for k in (1, 2, 3)
    ]
    mine = jnp.stack([g[0] for g in got])
    others = jnp.stack([g[1] for g in got])

    rows = jnp.transpose(queries[0].reshape(TOKENS, HEADS, HD), (1, 0, 2))
    pieces = rows.reshape(PIECES, PIECE, HD)
    spread = lax.all_to_all(pieces, "prompt", 0, 0, tiled=True)
    index = jnp.arange(PIECES, dtype=jnp.int32)
    server = jnp.sum(jnp.where(assignment[None, :] == index[:, None], index[None, :], 0), axis=1)
    sorted_in = jnp.take(spread, server, axis=0, mode="clip")
    home = lax.all_to_all(sorted_in, "prompt", 0, 0, tiled=True).reshape(ROWS, HD)

    part_c = lax.ppermute(others, "tp", swap(4))
    part_b = lax.ppermute(mine, "tp", swap(2))
    part_d = lax.ppermute(part_c, "tp", swap(2))
    far_a = lax.ppermute(mine, "tp", swap(1))
    far_b = lax.ppermute(part_b, "tp", swap(1))
    far_c = lax.ppermute(part_c, "tp", swap(1))
    far_d = lax.ppermute(part_d, "tp", swap(1))

    half = ROWS * 4096
    m, l, acc = call(
        first_kernel,
        [sds(ROWS, HD)] * 3,
        [home, mine, far_a, part_b, far_b],
        flops=4 * half * HD,
        exps=half,
    )
    done = call(
        second_kernel,
        [sds(PIECES, PIECE + EXTRA, HD, dtype=BF16)],
        [home, part_c, far_c, part_d, far_d, m, l, acc],
        scratch=[pltpu.VMEM((ROWS, HD), BF16), pltpu.VMEM((ROWS, HD), BF16)],
        flops=4 * half * HD,
        exps=half,
    )

    every = (mine, far_a, part_b, far_b, part_c, far_c, part_d, far_d)
    offsets = (0, 1, 2, 3, 4, 5, 6, 7)
    tail = jnp.stack([e[:, 2 * BLOCK :] for e in every])
    suf_k = tail[:, :, : 2 * STEPS].reshape(TOKENS, HD)
    suf_v = tail[:, :, 2 * STEPS : 4 * STEPS].reshape(TOKENS, HD)
    source = (
        8 * ((x - jnp.arange(4, dtype=jnp.int32)) % 4)[None, :]
        + ((tp % 8) ^ jnp.array(offsets, jnp.int32))[:, None]
    )
    shape = (8, 4, STEPS, 2)
    sample = 2 * source[:, :, None, None] + lax.broadcasted_iota(jnp.int32, shape, 3)
    step = lax.broadcasted_iota(jnp.int32, shape, 2)
    wide = (TOKENS, TOKENS)
    o_s, lse_s = call(
        suffix_kernel,
        [sds(ROWS, HD)] * 2,
        [
            rows.reshape(ROWS, HD),
            suf_k,
            suf_v,
            jnp.broadcast_to(step.reshape(1, TOKENS), wide),
            jnp.broadcast_to(sample.reshape(1, TOKENS), wide),
        ],
        flops=4 * ROWS * TOKENS * HD,
        exps=ROWS * TOKENS,
    )
    live = jnp.arange(STEPS, dtype=jnp.int32)[:, None] < suffix_lengths[0][None, :]
    live = jnp.broadcast_to(live.reshape(TOKENS, 1), (TOKENS, HD)).astype(jnp.int32)

    gone = lax.all_to_all(done, "prompt", 0, 0, tiled=True)
    sorted_out = jnp.take(gone, assignment, axis=0, mode="clip")
    back = lax.all_to_all(sorted_out, "prompt", 0, 0, tiled=True)
    out = call(
        merge_kernel, [sds(TOKENS, HEADS * HD, dtype=BF16)], [back, o_s, lse_s, live]
    )
    return out.reshape(1, STEPS, SAMPLES, HEADS * HD)


def solution(mesh):
    in_specs = (
        P("prompt", None, "tp", None),
        P("prompt", None, "tp", None),
        P("prompt", None, None, "tp"),
        P("prompt", None, "tp", None, None),
        P("prompt", None, "tp", None, None),
        P("prompt", None),
        P(),
    )
    out_specs = P("prompt", None, None, "tp")
    return jax.shard_map(local, mesh=mesh, in_specs=in_specs, out_specs=out_specs, check_vma=False)
```

```python
import functools
import math

import jax
import jax.numpy as jnp
from jax import lax
from jax.experimental import pallas as pl
from jax.experimental.pallas import tpu as pltpu
from jax.sharding import PartitionSpec as P

F32 = jnp.float32
BF16 = jnp.bfloat16
NEG = -1e30
VMEM = pl.BlockSpec(memory_space=pltpu.VMEM)

STEPS, SAMPLES, HD = 3, 64, 128
HEADS = 4
TOKENS = STEPS * SAMPLES
ROWS = HEADS * TOKENS
BLOCK = 256
SUF = 16
PART = 2 * BLOCK + SUF
HALF = 8 * BLOCK
HELD = 8 * PART
SORT_FLOPS = 40 * 10**9
PIECES = 16
PIECE = ROWS // PIECES
EXTRA = 8
SCALE2 = HD ** (-0.5) * math.log2(math.e)
TILE = 256


def dot_t(a, b):
    return lax.dot_general(a, b, (((1,), (1,)), ((), ())), preferred_element_type=F32)


def dot(a, b):
    return lax.dot_general(a, b, (((1,), (0,)), ((), ())), preferred_element_type=F32)


def split3(x):
    hi = x.astype(BF16)
    rest = x - hi.astype(F32)
    mid = rest.astype(BF16)
    low = (rest - mid.astype(F32)).astype(BF16)
    return hi, mid, low


def attend_tile(q, blocks, m, l, acc):
    scores = [dot_t(q, k[...]) for k, _ in blocks]
    top = functools.reduce(jnp.maximum, scores)
    m_new = jnp.maximum(m, jnp.max(top, axis=-1, keepdims=True) * SCALE2)
    fade = jnp.exp2(m - m_new)
    l = l * fade
    acc = acc * fade
    for s, (_, v) in zip(scores, blocks):
        w = jnp.exp2(s * SCALE2 - m_new)
        l = l + jnp.sum(w, axis=-1, keepdims=True)
        acc = acc + dot(w.astype(BF16), v[...])
    return m_new, l, acc


def sort_kernel(*refs):
    out = refs[-1]
    for n, (got, i) in enumerate((got, i) for got in refs[:-1] for i in range(2)):
        out[pl.ds(n * BLOCK, BLOCK)] = got[i, pl.ds(0, BLOCK)]
        out[pl.ds(HALF + n * BLOCK, BLOCK)] = got[i, pl.ds(BLOCK, BLOCK)]
        out[pl.ds(2 * HALF + n * SUF, SUF)] = got[i, pl.ds(2 * BLOCK, SUF)]


def views(ref):
    return [
        (ref.at[pl.ds(i, BLOCK)], ref.at[pl.ds(HALF + i, BLOCK)]) for i in range(0, HALF, BLOCK)
    ]


def attend(q, refs, state):
    blocks = [view for ref in refs for view in views(ref)]
    for i in range(0, len(blocks), 4):
        state = attend_tile(q, blocks[i : i + 4], *state)
    return state


def fresh_state():
    return (
        jnp.full((TILE, 1), NEG, F32),
        jnp.zeros((TILE, 1), F32),
        jnp.zeros((TILE, HD), F32),
    )


def tiles(body):
    def step(r, carry):
        body(pl.ds(pl.multiple_of(r * TILE, TILE), TILE))
        return carry

    lax.fori_loop(0, ROWS // TILE, step, 0)


def spread_out(column):
    return jnp.broadcast_to(column, (TILE, HD))


def result(m, l, acc):
    return acc / l, spread_out(m + jnp.log2(l))


def on_diagonal():
    row = lax.broadcasted_iota(jnp.int32, (PIECE, HD), 0)
    lane = lax.broadcasted_iota(jnp.int32, (PIECE, HD), 1)
    return row == lane


def pack(o, lse):
    line = jnp.sum(jnp.where(on_diagonal(), lse, 0.0), axis=0, keepdims=True)
    hi, mid, low = (jnp.broadcast_to(part.astype(F32), (EXTRA, HD)) for part in split3(line))
    row = lax.broadcasted_iota(jnp.int32, (EXTRA, HD), 0)
    parts = jnp.where(row == 0, hi, jnp.where(row == 1, mid, jnp.where(row == 2, low, 0.0)))
    return jnp.concatenate([o, parts], axis=0).astype(BF16)


def unpack(piece):
    piece = piece.astype(F32)
    line = jnp.sum(piece[PIECE:], axis=0, keepdims=True)
    lse = jnp.sum(jnp.where(on_diagonal(), line, 0.0), axis=1, keepdims=True)
    return piece[:PIECE], lse


def attend_kernel(q_ref, a, b, out_ref, o_sc, lse_sc):
    def body(at):
        o_sc[at], lse_sc[at] = result(*attend(q_ref[at], (a, b), fresh_state()))

    tiles(body)
    for p in range(PIECES):
        at = pl.ds(p * PIECE, PIECE)
        out_ref[p] = pack(o_sc[at], lse_sc[at])


def join(o1, lse1, o2, lse2):
    top = jnp.maximum(lse1, lse2)
    w1, w2 = jnp.exp2(lse1 - top), jnp.exp2(lse2 - top)
    total = w1 + w2
    return (w1 * o1 + w2 * o2) / total, top + jnp.log2(total)


def join_kernel(a_ref, b_ref, out_ref):
    for p in range(PIECES):
        out_ref[p] = pack(*join(*unpack(a_ref[p]), *unpack(b_ref[p])))


def suffix_kernel(q_ref, k_ref, v_ref, step_ref, sample_ref, o_ref, lse_ref):
    row = lax.broadcasted_iota(jnp.int32, (TOKENS, TOKENS), 0)
    keep = (sample_ref[...] == row % SAMPLES) & (step_ref[...] <= row // SAMPLES)
    for j in range(HEADS):
        at = pl.ds(j * TOKENS, TOKENS)
        t = jnp.where(keep, dot_t(q_ref[at], k_ref[...]) * SCALE2, NEG)
        m = jnp.max(t, axis=-1, keepdims=True)
        w = jnp.where(keep, jnp.exp2(t - m), 0.0)
        l = jnp.sum(w, axis=-1, keepdims=True)
        o_ref[at] = dot(w.astype(BF16), v_ref[...]) / l
        lse_ref[at] = jnp.broadcast_to(m + jnp.log2(l), (TOKENS, HD))


def merge_kernel(r_ref, o_ref, lse_ref, live_ref, out_ref):
    per_head = PIECES // HEADS
    for p in range(PIECES):
        at = pl.ds(p * PIECE, PIECE)
        tok = pl.ds((p % per_head) * PIECE, PIECE)
        merged, _ = join(o_ref[at], lse_ref[at], *unpack(r_ref[p]))
        merged = jnp.where(live_ref[tok] > 0, merged, 0.0)
        out_ref[tok, pl.ds((p // per_head) * HD, HD)] = merged.astype(BF16)


def call(kernel, outs, args, scratch=(), flops=0, exps=0):
    moved = sum(math.prod(a.shape) * a.dtype.itemsize for a in (*args, *outs))
    many = len(outs) > 1
    return pl.pallas_call(
        kernel,
        out_shape=tuple(outs) if many else outs[0],
        in_specs=[VMEM] * len(args),
        out_specs=(VMEM,) * len(outs) if many else VMEM,
        scratch_shapes=list(scratch),
        compiler_params=pltpu.CompilerParams(vmem_limit_bytes=40 * 2**20),
        cost_estimate=pl.CostEstimate(flops=flops, bytes_accessed=moved, transcendentals=exps),
    )(*args)


def sds(*shape, dtype=F32):
    return jax.ShapeDtypeStruct(shape, dtype)


def local(
    prompt_keys, prompt_values, queries, sample_step_keys, suffix_values, suffix_lengths, assignment
):
    tp = lax.axis_index("tp")
    x, z, core = tp // 8, (tp // 2) % 4, tp % 2
    keys, values = prompt_keys[0], prompt_values[0]

    def turn(zz):
        return (zz % 2) * 2 + zz // 2

    def permute(a, target):
        pairs = []
        for t in range(32):
            to_x, to_z, to_core = target(t // 8, (t // 2) % 4, t % 2)
            pairs.append((t, 8 * to_x + 2 * to_z + to_core))
        return lax.ppermute(a, "tp", pairs)

    def there_0(xx, zz, cc):
        return xx, turn(zz), cc

    def there_1(xx, zz, cc):
        return xx, turn(zz) ^ 2, cc

    def back_1(xx, zz, cc):
        return xx, turn(zz ^ 2), cc

    fresh = jnp.stack([sample_step_keys[0], suffix_values[0]])
    fresh = jnp.transpose(fresh, (3, 0, 1, 2, 4)).reshape(8, 4 * STEPS, HD)
    fresh = jnp.pad(fresh, ((0, 0), (0, SUF - 4 * STEPS), (0, 0)))

    def of_parity(which):
        parts = [
            lax.dynamic_index_in_dim(a.reshape(4, 2, -1, HD), which, 1, keepdims=False)
            for a in (keys, values, fresh)
        ]
        return jnp.concatenate(parts, axis=1)

    rows = jnp.transpose(queries[0].reshape(TOKENS, HEADS, HD), (1, 0, 2))
    pieces = rows.reshape(PIECES, PIECE, HD)
    spread = lax.all_to_all(pieces, "prompt", 0, 0, tiled=True)
    index = jnp.arange(PIECES, dtype=jnp.int32)
    server = jnp.sum(jnp.where(assignment[None, :] == index[:, None], index[None, :], 0), axis=1)
    sorted_in = jnp.take(spread, server, axis=0, mode="clip")
    kept = of_parity(z % 2)
    came = permute(of_parity(1 - z % 2), lambda xx, zz, cc: (xx, zz ^ 1, cc))

    def payload(to):
        return jnp.stack(
            [lax.dynamic_index_in_dim(a, to, 0, keepdims=False) for a in (kept, came)]
        )

    got = [payload(x)]
    for k in (1, 2, 3):
        shift = lambda xx, zz, cc, k=k: ((xx + k) % 4, zz, cc)
        got.append(permute(payload((x + k) % 4), shift))
    mine = call(sort_kernel, [sds(HELD, HD, dtype=BF16)], got, flops=SORT_FLOPS)
    home = lax.all_to_all(sorted_in, "prompt", 0, 0, tiled=True).reshape(ROWS, HD)
    mine, home = lax.optimization_barrier((mine, home))
    far = permute(mine, lambda xx, zz, cc: (xx, zz, cc ^ 1))

    def cost(positions):
        return dict(flops=4 * ROWS * positions * HD, exps=ROWS * positions)

    held = [mine, far]
    packed = sds(PIECES, PIECE + EXTRA, HD, dtype=BF16)
    wide = pltpu.VMEM((ROWS, HD), F32)
    partial = []
    for there, back in ((there_0, there_0), (there_1, back_1)):
        part = call(
            attend_kernel,
            [packed],
            [permute(home, there), *held],
            scratch=[wide, wide],
            **cost(4096),
        )
        partial.append(permute(part, back))
    done = call(join_kernel, [packed], partial)

    done, held = lax.optimization_barrier((done, held))
    tail = jnp.stack([e[2 * HALF :].reshape(8, SUF, HD) for e in held])
    tail = jnp.stack([permute(tail, there_0), permute(tail, back_1)])
    live = jnp.arange(STEPS, dtype=jnp.int32)[:, None] < suffix_lengths[0][None, :]
    live = jnp.broadcast_to(live.reshape(TOKENS, 1), (TOKENS, HD)).astype(jnp.int32)

    gone = lax.all_to_all(done, "prompt", 0, 0, tiled=True)
    gone, tail = lax.optimization_barrier((gone, tail))
    sorted_out = jnp.take(gone, assignment, axis=0, mode="clip")
    sorted_out, tail = lax.optimization_barrier((sorted_out, tail))
    suf_k = tail[:, :, :, : 2 * STEPS].reshape(TOKENS, HD)
    suf_v = tail[:, :, :, 2 * STEPS : 4 * STEPS].reshape(TOKENS, HD)
    shape = (2, 2, 4, 2, STEPS, 2)
    at = [lax.broadcasted_iota(jnp.int32, shape, d) for d in range(6)]
    origin = turn(z) ^ (2 * at[0])
    source = 8 * ((x - at[2]) % 4) + 2 * (origin ^ at[3]) + (core ^ at[1])
    sample, step = 2 * source + at[5], at[4]
    wide = (TOKENS, TOKENS)
    o_s, lse_s = call(
        suffix_kernel,
        [sds(ROWS, HD)] * 2,
        [
            rows.reshape(ROWS, HD),
            suf_k,
            suf_v,
            jnp.broadcast_to(step.reshape(1, TOKENS), wide),
            jnp.broadcast_to(sample.reshape(1, TOKENS), wide),
        ],
        flops=4 * ROWS * TOKENS * HD,
        exps=ROWS * TOKENS,
    )
    back = lax.all_to_all(sorted_out, "prompt", 0, 0, tiled=True)
    out = call(
        merge_kernel, [sds(TOKENS, HEADS * HD, dtype=BF16)], [back, o_s, lse_s, live]
    )
    return out.reshape(1, STEPS, SAMPLES, HEADS * HD)


def solution(mesh):
    in_specs = (
        P("prompt", None, "tp", None),
        P("prompt", None, "tp", None),
        P("prompt", None, None, "tp"),
        P("prompt", None, "tp", None, None),
        P("prompt", None, "tp", None, None),
        P("prompt", None),
        P(),
    )
    out_specs = P("prompt", None, None, "tp")
    return jax.shard_map(local, mesh=mesh, in_specs=in_specs, out_specs=out_specs, check_vma=False)
```

```python
import functools
import math

import jax
import jax.numpy as jnp
from jax import lax
from jax.experimental import pallas as pl
from jax.experimental.pallas import tpu as pltpu
from jax.sharding import PartitionSpec as P

F32 = jnp.float32
BF16 = jnp.bfloat16
NEG = -1e30
VMEM = pl.BlockSpec(memory_space=pltpu.VMEM)

STEPS, SAMPLES, HD = 3, 64, 128
HEADS = 4
TOKENS = STEPS * SAMPLES
ROWS = HEADS * TOKENS
BLOCK = 256
SUF = 16
PART = 2 * BLOCK + SUF
HALF = 8 * BLOCK
SORT_FLOPS = 40 * 10**9
PIECES = 16
PIECE = ROWS // PIECES
EXTRA = 8
SCALE2 = HD ** (-0.5) * math.log2(math.e)
CHUNK = 1024


def dot_t(a, b):
    return lax.dot_general(a, b, (((1,), (1,)), ((), ())), preferred_element_type=F32)


def dot(a, b):
    return lax.dot_general(a, b, (((1,), (0,)), ((), ())), preferred_element_type=F32)


def split3(x):
    hi = x.astype(BF16)
    rest = x - hi.astype(F32)
    mid = rest.astype(BF16)
    low = (rest - mid.astype(F32)).astype(BF16)
    return hi, mid, low


def attend(q, held):
    m = jnp.full((ROWS, 1), NEG, F32)
    l = jnp.zeros((ROWS, 1), F32)
    acc = jnp.zeros((ROWS, HD), F32)
    for keys, values in held:
        for i in range(0, HALF, CHUNK):
            at = pl.ds(i, CHUNK)
            s = dot_t(q, keys[at])
            m_new = jnp.maximum(m, jnp.max(s, axis=-1, keepdims=True) * SCALE2)
            fade = jnp.exp2(m - m_new)
            w = jnp.exp2(s * SCALE2 - m_new)
            l = l * fade + jnp.sum(w, axis=-1, keepdims=True)
            acc = acc * fade + dot(w.astype(BF16), values[at])
            m = m_new
    return acc / l, m + jnp.log2(l)


def sort_kernel(*refs):
    *blocks, keys, rest = refs
    for n, (got, i) in enumerate((got, i) for got in blocks for i in range(2)):
        keys[pl.ds(n * BLOCK, BLOCK)] = got[i, pl.ds(0, BLOCK)]
        rest[pl.ds(n * BLOCK, BLOCK)] = got[i, pl.ds(BLOCK, BLOCK)]
        rest[pl.ds(HALF + n * SUF, SUF)] = got[i, pl.ds(2 * BLOCK, SUF)]


def on_diagonal():
    row = lax.broadcasted_iota(jnp.int32, (PIECE, HD), 0)
    lane = lax.broadcasted_iota(jnp.int32, (PIECE, HD), 1)
    return row == lane


def pack(o, lse):
    line = jnp.sum(jnp.where(on_diagonal(), lse, 0.0), axis=0, keepdims=True)
    hi, mid, low = (jnp.broadcast_to(part.astype(F32), (EXTRA, HD)) for part in split3(line))
    row = lax.broadcasted_iota(jnp.int32, (EXTRA, HD), 0)
    parts = jnp.where(row == 0, hi, jnp.where(row == 1, mid, jnp.where(row == 2, low, 0.0)))
    return jnp.concatenate([o, parts], axis=0).astype(BF16)


def pack_wide(o, lse):
    line = jnp.sum(jnp.where(on_diagonal(), lse, 0.0), axis=0, keepdims=True)
    row = lax.broadcasted_iota(jnp.int32, (EXTRA, HD), 0)
    return jnp.concatenate([o, jnp.where(row == 0, line, 0.0)], axis=0)


def unpack(piece):
    piece = piece.astype(F32)
    line = jnp.sum(piece[PIECE:], axis=0, keepdims=True)
    lse = jnp.sum(jnp.where(on_diagonal(), line, 0.0), axis=1, keepdims=True)
    return piece[:PIECE], lse


def attend_kernel(q_ref, k_a, v_a, k_b, v_b, out_ref, o_sc, lse_sc):
    o_sc[...], lse = attend(q_ref[...], ((k_a, v_a), (k_b, v_b)))
    lse_sc[...] = jnp.broadcast_to(lse, (ROWS, HD))
    code = pack if out_ref.dtype == BF16 else pack_wide
    for p in range(PIECES):
        at = pl.ds(p * PIECE, PIECE)
        out_ref[p] = code(o_sc[at], lse_sc[at])


def join(o1, lse1, o2, lse2):
    top = jnp.maximum(lse1, lse2)
    w1, w2 = jnp.exp2(lse1 - top), jnp.exp2(lse2 - top)
    total = w1 + w2
    return (w1 * o1 + w2 * o2) / total, top + jnp.log2(total)


def join_kernel(a_ref, b_ref, out_ref):
    for p in range(PIECES):
        out_ref[p] = pack(*join(*unpack(a_ref[p]), *unpack(b_ref[p])))


def suffix_kernel(q_ref, k_ref, v_ref, step_ref, sample_ref, o_ref, lse_ref):
    row = lax.broadcasted_iota(jnp.int32, (TOKENS, TOKENS), 0)
    keep = (sample_ref[...] == row % SAMPLES) & (step_ref[...] <= row // SAMPLES)
    for j in range(HEADS):
        at = pl.ds(j * TOKENS, TOKENS)
        t = jnp.where(keep, dot_t(q_ref[at], k_ref[...]) * SCALE2, NEG)
        m = jnp.max(t, axis=-1, keepdims=True)
        w = jnp.where(keep, jnp.exp2(t - m), 0.0)
        l = jnp.sum(w, axis=-1, keepdims=True)
        o_ref[at] = dot(w.astype(BF16), v_ref[...]) / l
        lse_ref[at] = jnp.broadcast_to(m + jnp.log2(l), (TOKENS, HD))


def merge_kernel(r_ref, o_ref, lse_ref, live_ref, out_ref):
    per_head = PIECES // HEADS
    for p in range(PIECES):
        at = pl.ds(p * PIECE, PIECE)
        tok = pl.ds((p % per_head) * PIECE, PIECE)
        merged, _ = join(o_ref[at], lse_ref[at], *unpack(r_ref[p]))
        merged = jnp.where(live_ref[tok] > 0, merged, 0.0)
        out_ref[tok, pl.ds((p // per_head) * HD, HD)] = merged.astype(BF16)


def call(kernel, outs, args, scratch=(), flops=0, exps=0):
    moved = sum(math.prod(a.shape) * a.dtype.itemsize for a in (*args, *outs))
    many = len(outs) > 1
    return pl.pallas_call(
        kernel,
        out_shape=tuple(outs) if many else outs[0],
        in_specs=[VMEM] * len(args),
        out_specs=(VMEM,) * len(outs) if many else VMEM,
        scratch_shapes=list(scratch),
        compiler_params=pltpu.CompilerParams(vmem_limit_bytes=40 * 2**20),
        cost_estimate=pl.CostEstimate(flops=flops, bytes_accessed=moved, transcendentals=exps),
    )(*args)


def sds(*shape, dtype=F32):
    return jax.ShapeDtypeStruct(shape, dtype)


def local(
    prompt_keys, prompt_values, queries, sample_step_keys, suffix_values, suffix_lengths, assignment
):
    tp = lax.axis_index("tp")
    x, z, core = tp // 8, (tp // 2) % 4, tp % 2
    keys, values = prompt_keys[0], prompt_values[0]

    def turn(zz):
        return (zz % 2) * 2 + zz // 2

    def permute(a, target):
        pairs = []
        for t in range(32):
            to_x, to_z, to_core = target(t // 8, (t // 2) % 4, t % 2)
            pairs.append((t, 8 * to_x + 2 * to_z + to_core))
        return lax.ppermute(a, "tp", pairs)

    def there_0(xx, zz, cc):
        return xx, turn(zz), cc

    def there_1(xx, zz, cc):
        return xx, turn(zz) ^ 2, cc

    def back_1(xx, zz, cc):
        return xx, turn(zz ^ 2), cc

    fresh = jnp.stack([sample_step_keys[0], suffix_values[0]])
    fresh = jnp.transpose(fresh, (3, 0, 1, 2, 4)).reshape(8, 4 * STEPS, HD)
    fresh = jnp.pad(fresh, ((0, 0), (0, SUF - 4 * STEPS), (0, 0)))

    def of_parity(which):
        parts = [
            lax.dynamic_index_in_dim(a.reshape(4, 2, -1, HD), which, 1, keepdims=False)
            for a in (keys, values, fresh)
        ]
        return jnp.concatenate(parts, axis=1)

    rows = jnp.transpose(queries[0].reshape(TOKENS, HEADS, HD), (1, 0, 2))
    pieces = rows.reshape(PIECES, PIECE, HD)
    spread = lax.all_to_all(pieces, "prompt", 0, 0, tiled=True)
    index = jnp.arange(PIECES, dtype=jnp.int32)
    server = jnp.sum(jnp.where(assignment[None, :] == index[:, None], index[None, :], 0), axis=1)
    sorted_in = jnp.take(spread, server, axis=0, mode="clip")
    kept = of_parity(z % 2)
    came = permute(of_parity(1 - z % 2), lambda xx, zz, cc: (xx, zz ^ 1, cc))

    def payload(to):
        return jnp.stack(
            [lax.dynamic_index_in_dim(a, to, 0, keepdims=False) for a in (kept, came)]
        )

    got = [payload(x)]
    for k in (1, 2, 3):
        shift = lambda xx, zz, cc, k=k: ((xx + k) % 4, zz, cc)
        got.append(permute(payload((x + k) % 4), shift))
    mine = call(
        sort_kernel,
        [sds(HALF, HD, dtype=BF16), sds(HALF + 8 * SUF, HD, dtype=BF16)],
        got,
        flops=SORT_FLOPS,
    )
    home = lax.all_to_all(sorted_in, "prompt", 0, 0, tiled=True).reshape(ROWS, HD)
    far = [permute(a, lambda xx, zz, cc: (xx, zz, cc ^ 1)) for a in mine]

    def cost(positions):
        return dict(flops=4 * ROWS * positions * HD, exps=ROWS * positions)

    held = [*mine, *far]
    wide = pltpu.VMEM((ROWS, HD), F32)
    partial = []
    for there, back, kind in ((there_0, there_0, BF16), (there_1, back_1, F32)):
        part = call(
            attend_kernel,
            [sds(PIECES, PIECE + EXTRA, HD, dtype=kind)],
            [permute(home, there), *held],
            scratch=[wide, wide],
            **cost(4096),
        )
        partial.append(permute(part, back))
    done = call(join_kernel, [sds(PIECES, PIECE + EXTRA, HD, dtype=BF16)], partial)

    tail = jnp.stack([e[1][HALF:].reshape(8, SUF, HD) for e in (mine, far)])
    done, tail = lax.optimization_barrier((done, tail))
    tail = jnp.stack([permute(tail, there_0), permute(tail, back_1)])
    live = jnp.arange(STEPS, dtype=jnp.int32)[:, None] < suffix_lengths[0][None, :]
    live = jnp.broadcast_to(live.reshape(TOKENS, 1), (TOKENS, HD)).astype(jnp.int32)

    gone = lax.all_to_all(done, "prompt", 0, 0, tiled=True)
    gone, tail = lax.optimization_barrier((gone, tail))
    sorted_out = jnp.take(gone, assignment, axis=0, mode="clip")
    sorted_out, tail = lax.optimization_barrier((sorted_out, tail))
    suf_k = tail[:, :, :, : 2 * STEPS].reshape(TOKENS, HD)
    suf_v = tail[:, :, :, 2 * STEPS : 4 * STEPS].reshape(TOKENS, HD)
    shape = (2, 2, 4, 2, STEPS, 2)
    at = [lax.broadcasted_iota(jnp.int32, shape, d) for d in range(6)]
    origin = turn(z) ^ (2 * at[0])
    source = 8 * ((x - at[2]) % 4) + 2 * (origin ^ at[3]) + (core ^ at[1])
    sample, step = 2 * source + at[5], at[4]
    wide = (TOKENS, TOKENS)
    o_s, lse_s = call(
        suffix_kernel,
        [sds(ROWS, HD)] * 2,
        [
            rows.reshape(ROWS, HD),
            suf_k,
            suf_v,
            jnp.broadcast_to(step.reshape(1, TOKENS), wide),
            jnp.broadcast_to(sample.reshape(1, TOKENS), wide),
        ],
        flops=4 * ROWS * TOKENS * HD,
        exps=ROWS * TOKENS,
    )
    back = lax.all_to_all(sorted_out, "prompt", 0, 0, tiled=True)
    out = call(
        merge_kernel, [sds(TOKENS, HEADS * HD, dtype=BF16)], [back, o_s, lse_s, live]
    )
    return out.reshape(1, STEPS, SAMPLES, HEADS * HD)


def solution(mesh):
    in_specs = (
        P("prompt", None, "tp", None),
        P("prompt", None, "tp", None),
        P("prompt", None, None, "tp"),
        P("prompt", None, "tp", None, None),
        P("prompt", None, "tp", None, None),
        P("prompt", None),
        P(),
    )
    out_specs = P("prompt", None, None, "tp")
    return jax.shard_map(local, mesh=mesh, in_specs=in_specs, out_specs=out_specs, check_vma=False)
```

```python
import functools
import math

import jax
import jax.numpy as jnp
from jax import lax
from jax.experimental import pallas as pl
from jax.experimental.pallas import tpu as pltpu
from jax.sharding import PartitionSpec as P

F32 = jnp.float32
BF16 = jnp.bfloat16
NEG = -1e30
VMEM = pl.BlockSpec(memory_space=pltpu.VMEM)

STEPS, SAMPLES, HD = 3, 64, 128
HEADS = 4
TOKENS = STEPS * SAMPLES
ROWS = HEADS * TOKENS
BLOCK = 256
SUF = 16
PART = 2 * BLOCK + SUF
HALF = 8 * BLOCK
SORT_FLOPS = 40 * 10**9
PIECES = 16
PIECE = ROWS // PIECES
EXTRA = 8
LANES = 128
UNITS = ROWS // LANES
PACKED = ROWS + 32
PACKED_WIDE = ROWS + 8
SCALE2 = HD ** (-0.5) * math.log2(math.e)
CHUNK = 1024


def dot_t(a, b):
    return lax.dot_general(a, b, (((1,), (1,)), ((), ())), preferred_element_type=F32)


def dot(a, b):
    return lax.dot_general(a, b, (((1,), (0,)), ((), ())), preferred_element_type=F32)


def split3(x):
    hi = x.astype(BF16)
    rest = x - hi.astype(F32)
    mid = rest.astype(BF16)
    low = (rest - mid.astype(F32)).astype(BF16)
    return hi, mid, low


def attend(q, held):
    m = jnp.full((ROWS, 1), NEG, F32)
    l = jnp.zeros((ROWS, 1), F32)
    acc = jnp.zeros((ROWS, HD), F32)
    for keys, values in held:
        for i in range(0, HALF, CHUNK):
            at = pl.ds(i, CHUNK)
            s = dot_t(q, keys[at])
            m_new = jnp.maximum(m, jnp.max(s, axis=-1, keepdims=True) * SCALE2)
            fade = jnp.exp2(m - m_new)
            w = jnp.exp2(s * SCALE2 - m_new)
            l = l * fade + jnp.sum(w, axis=-1, keepdims=True)
            acc = acc * fade + dot(w.astype(BF16), values[at])
            m = m_new
    return acc / l, m + jnp.log2(l)


def sort_kernel(*refs):
    *blocks, keys, rest = refs
    for n, (got, i) in enumerate((got, i) for got in blocks for i in range(2)):
        keys[pl.ds(n * BLOCK, BLOCK)] = got[i, pl.ds(0, BLOCK)]
        rest[pl.ds(n * BLOCK, BLOCK)] = got[i, pl.ds(BLOCK, BLOCK)]
        rest[pl.ds(HALF + n * SUF, SUF)] = got[i, pl.ds(2 * BLOCK, SUF)]


def on_diagonal(rows):
    row = lax.broadcasted_iota(jnp.int32, (rows, LANES), 0)
    return row == lax.broadcasted_iota(jnp.int32, (rows, LANES), 1)


def unit(u):
    return pl.ds(u * LANES, LANES)


def to_line(column):
    return jnp.sum(jnp.where(on_diagonal(column.shape[0]), column, 0.0), axis=0, keepdims=True)


def to_column(line, rows):
    return jnp.sum(jnp.where(on_diagonal(rows), line, 0.0), axis=1, keepdims=True)


def store_lines(out_ref, lines):
    lines = jnp.concatenate(lines + [jnp.zeros((8 - UNITS, LANES), F32)], axis=0)
    if out_ref.dtype == BF16:
        parts = [part.astype(F32) for part in split3(lines)]
        lines = jnp.concatenate(parts + [jnp.zeros((8, LANES), F32)], axis=0).astype(BF16)
    out_ref[pl.ds(ROWS, lines.shape[0])] = lines


def load_lines(ref):
    if ref.dtype == BF16:
        parts = ref[pl.ds(ROWS, PACKED - ROWS)].astype(F32)
        return parts[0:8] + parts[8:16] + parts[16:24]
    return ref[pl.ds(ROWS, PACKED_WIDE - ROWS)]


def pack(o, lse):
    line = to_line(lse)
    hi, mid, low = (jnp.broadcast_to(part.astype(F32), (EXTRA, HD)) for part in split3(line))
    row = lax.broadcasted_iota(jnp.int32, (EXTRA, HD), 0)
    parts = jnp.where(row == 0, hi, jnp.where(row == 1, mid, jnp.where(row == 2, low, 0.0)))
    return jnp.concatenate([o, parts], axis=0).astype(BF16)


def unpack(piece):
    piece = piece.astype(F32)
    line = jnp.sum(piece[PIECE:], axis=0, keepdims=True)
    return piece[:PIECE], to_column(line, PIECE)


def attend_kernel(q_ref, k_a, v_a, k_b, v_b, out_ref, lse_sc):
    o, lse = attend(q_ref[...], ((k_a, v_a), (k_b, v_b)))
    out_ref[pl.ds(0, ROWS)] = o.astype(out_ref.dtype)
    lse_sc[...] = jnp.broadcast_to(lse, (ROWS, LANES))
    store_lines(out_ref, [to_line(lse_sc[unit(u)]) for u in range(UNITS)])


def join(o1, lse1, o2, lse2):
    top = jnp.maximum(lse1, lse2)
    w1, w2 = jnp.exp2(lse1 - top), jnp.exp2(lse2 - top)
    total = w1 + w2
    return (w1 * o1 + w2 * o2) / total, top + jnp.log2(total)


def join_kernel(a_ref, b_ref, out_ref, o_sc, lse_sc):
    lines_a, lines_b = load_lines(a_ref), load_lines(b_ref)
    for u in range(UNITS):
        lse_a, lse_b = (to_column(lines[u : u + 1], LANES) for lines in (lines_a, lines_b))
        o, lse = join(a_ref[unit(u)].astype(F32), lse_a, b_ref[unit(u)].astype(F32), lse_b)
        o_sc[unit(u)] = o
        lse_sc[unit(u)] = jnp.broadcast_to(lse, (LANES, LANES))
    for p in range(PIECES):
        at = pl.ds(p * PIECE, PIECE)
        out_ref[p] = pack(o_sc[at], lse_sc[at])


def suffix_kernel(q_ref, k_ref, v_ref, step_ref, sample_ref, o_ref, lse_ref):
    row = lax.broadcasted_iota(jnp.int32, (TOKENS, TOKENS), 0)
    keep = (sample_ref[...] == row % SAMPLES) & (step_ref[...] <= row // SAMPLES)
    for j in range(HEADS):
        at = pl.ds(j * TOKENS, TOKENS)
        t = jnp.where(keep, dot_t(q_ref[at], k_ref[...]) * SCALE2, NEG)
        m = jnp.max(t, axis=-1, keepdims=True)
        w = jnp.where(keep, jnp.exp2(t - m), 0.0)
        l = jnp.sum(w, axis=-1, keepdims=True)
        o_ref[at] = dot(w.astype(BF16), v_ref[...]) / l
        lse_ref[at] = jnp.broadcast_to(m + jnp.log2(l), (TOKENS, HD))


def merge_kernel(r_ref, o_ref, lse_ref, live_ref, out_ref):
    per_head = PIECES // HEADS
    for p in range(PIECES):
        at = pl.ds(p * PIECE, PIECE)
        tok = pl.ds((p % per_head) * PIECE, PIECE)
        merged, _ = join(o_ref[at], lse_ref[at], *unpack(r_ref[p]))
        merged = jnp.where(live_ref[tok] > 0, merged, 0.0)
        out_ref[tok, pl.ds((p // per_head) * HD, HD)] = merged.astype(BF16)


def call(kernel, outs, args, scratch=(), flops=0, exps=0):
    moved = sum(math.prod(a.shape) * a.dtype.itemsize for a in (*args, *outs))
    many = len(outs) > 1
    return pl.pallas_call(
        kernel,
        out_shape=tuple(outs) if many else outs[0],
        in_specs=[VMEM] * len(args),
        out_specs=(VMEM,) * len(outs) if many else VMEM,
        scratch_shapes=list(scratch),
        compiler_params=pltpu.CompilerParams(vmem_limit_bytes=40 * 2**20),
        cost_estimate=pl.CostEstimate(flops=flops, bytes_accessed=moved, transcendentals=exps),
    )(*args)


def sds(*shape, dtype=F32):
    return jax.ShapeDtypeStruct(shape, dtype)


def local(
    prompt_keys, prompt_values, queries, sample_step_keys, suffix_values, suffix_lengths, assignment
):
    tp = lax.axis_index("tp")
    x, z, core = tp // 8, (tp // 2) % 4, tp % 2
    keys, values = prompt_keys[0], prompt_values[0]

    def turn(zz):
        return (zz % 2) * 2 + zz // 2

    def permute(a, target):
        pairs = []
        for t in range(32):
            to_x, to_z, to_core = target(t // 8, (t // 2) % 4, t % 2)
            pairs.append((t, 8 * to_x + 2 * to_z + to_core))
        return lax.ppermute(a, "tp", pairs)

    def there_0(xx, zz, cc):
        return xx, turn(zz), cc

    def there_1(xx, zz, cc):
        return xx, turn(zz) ^ 2, cc

    def back_1(xx, zz, cc):
        return xx, turn(zz ^ 2), cc

    fresh = jnp.stack([sample_step_keys[0], suffix_values[0]])
    fresh = jnp.transpose(fresh, (3, 0, 1, 2, 4)).reshape(8, 4 * STEPS, HD)
    fresh = jnp.pad(fresh, ((0, 0), (0, SUF - 4 * STEPS), (0, 0)))

    def of_parity(which):
        parts = [
            lax.dynamic_index_in_dim(a.reshape(4, 2, -1, HD), which, 1, keepdims=False)
            for a in (keys, values, fresh)
        ]
        return jnp.concatenate(parts, axis=1)

    rows = jnp.transpose(queries[0].reshape(TOKENS, HEADS, HD), (1, 0, 2))
    pieces = rows.reshape(PIECES, PIECE, HD)
    spread = lax.all_to_all(pieces, "prompt", 0, 0, tiled=True)
    index = jnp.arange(PIECES, dtype=jnp.int32)
    server = jnp.sum(jnp.where(assignment[None, :] == index[:, None], index[None, :], 0), axis=1)
    sorted_in = jnp.take(spread, server, axis=0, mode="clip")
    kept = of_parity(z % 2)
    came = permute(of_parity(1 - z % 2), lambda xx, zz, cc: (xx, zz ^ 1, cc))

    def payload(to):
        return jnp.stack(
            [lax.dynamic_index_in_dim(a, to, 0, keepdims=False) for a in (kept, came)]
        )

    got = [payload(x)]
    for k in (1, 2, 3):
        shift = lambda xx, zz, cc, k=k: ((xx + k) % 4, zz, cc)
        got.append(permute(payload((x + k) % 4), shift))
    mine = call(
        sort_kernel,
        [sds(HALF, HD, dtype=BF16), sds(HALF + 8 * SUF, HD, dtype=BF16)],
        got,
        flops=SORT_FLOPS,
    )
    home = lax.all_to_all(sorted_in, "prompt", 0, 0, tiled=True).reshape(ROWS, HD)
    far = [permute(a, lambda xx, zz, cc: (xx, zz, cc ^ 1)) for a in mine]

    def cost(positions):
        return dict(flops=4 * ROWS * positions * HD, exps=ROWS * positions)

    held = [*mine, *far]
    wide = pltpu.VMEM((ROWS, HD), F32)
    partial = []
    for there, back, kind, size in (
        (there_0, there_0, BF16, PACKED),
        (there_1, back_1, F32, PACKED_WIDE),
    ):
        part = call(
            attend_kernel,
            [sds(size, HD, dtype=kind)],
            [permute(home, there), *held],
            scratch=[wide],
            **cost(4096),
        )
        partial.append(permute(part, back))
    done = call(
        join_kernel, [sds(PIECES, PIECE + EXTRA, HD, dtype=BF16)], partial, scratch=[wide, wide]
    )

    tail = jnp.stack([e[1][HALF:].reshape(8, SUF, HD) for e in (mine, far)])
    done, tail = lax.optimization_barrier((done, tail))
    tail = jnp.stack([permute(tail, there_0), permute(tail, back_1)])
    live = jnp.arange(STEPS, dtype=jnp.int32)[:, None] < suffix_lengths[0][None, :]
    live = jnp.broadcast_to(live.reshape(TOKENS, 1), (TOKENS, HD)).astype(jnp.int32)

    gone = lax.all_to_all(done, "prompt", 0, 0, tiled=True)
    gone, tail = lax.optimization_barrier((gone, tail))
    sorted_out = jnp.take(gone, assignment, axis=0, mode="clip")
    sorted_out, tail = lax.optimization_barrier((sorted_out, tail))
    suf_k = tail[:, :, :, : 2 * STEPS].reshape(TOKENS, HD)
    suf_v = tail[:, :, :, 2 * STEPS : 4 * STEPS].reshape(TOKENS, HD)
    shape = (2, 2, 4, 2, STEPS, 2)
    at = [lax.broadcasted_iota(jnp.int32, shape, d) for d in range(6)]
    origin = turn(z) ^ (2 * at[0])
    source = 8 * ((x - at[2]) % 4) + 2 * (origin ^ at[3]) + (core ^ at[1])
    sample, step = 2 * source + at[5], at[4]
    wide = (TOKENS, TOKENS)
    o_s, lse_s = call(
        suffix_kernel,
        [sds(ROWS, HD)] * 2,
        [
            rows.reshape(ROWS, HD),
            suf_k,
            suf_v,
            jnp.broadcast_to(step.reshape(1, TOKENS), wide),
            jnp.broadcast_to(sample.reshape(1, TOKENS), wide),
        ],
        flops=4 * ROWS * TOKENS * HD,
        exps=ROWS * TOKENS,
    )
    back = lax.all_to_all(sorted_out, "prompt", 0, 0, tiled=True)
    out = call(
        merge_kernel, [sds(TOKENS, HEADS * HD, dtype=BF16)], [back, o_s, lse_s, live]
    )
    return out.reshape(1, STEPS, SAMPLES, HEADS * HD)


def solution(mesh):
    in_specs = (
        P("prompt", None, "tp", None),
        P("prompt", None, "tp", None),
        P("prompt", None, None, "tp"),
        P("prompt", None, "tp", None, None),
        P("prompt", None, "tp", None, None),
        P("prompt", None),
        P(),
    )
    out_specs = P("prompt", None, None, "tp")
    return jax.shard_map(local, mesh=mesh, in_specs=in_specs, out_specs=out_specs, check_vma=False)
```

```python
import functools
import math

import jax
import jax.numpy as jnp
from jax import lax
from jax.experimental import pallas as pl
from jax.experimental.pallas import tpu as pltpu
from jax.sharding import PartitionSpec as P

F32 = jnp.float32
BF16 = jnp.bfloat16
NEG = -1e30
VMEM = pl.BlockSpec(memory_space=pltpu.VMEM)

STEPS, SAMPLES, HD = 3, 64, 128
HEADS = 4
TOKENS = STEPS * SAMPLES
ROWS = HEADS * TOKENS
BLOCK = 256
SUF = 16
PART = 2 * BLOCK + SUF
HALF = 8 * BLOCK
SORT_FLOPS = 40 * 10**9
PIECES = 16
PIECE = ROWS // PIECES
EXTRA = 8
LANES = 128
UNITS = ROWS // LANES
PACKED = ROWS + 32
PACKED_WIDE = ROWS + 8
SCALE2 = HD ** (-0.5) * math.log2(math.e)
CHUNK = 1024
FIRST = 10


def dot_t(a, b):
    return lax.dot_general(a, b, (((1,), (1,)), ((), ())), preferred_element_type=F32)


def dot(a, b):
    return lax.dot_general(a, b, (((1,), (0,)), ((), ())), preferred_element_type=F32)


def split3(x):
    hi = x.astype(BF16)
    rest = x - hi.astype(F32)
    mid = rest.astype(BF16)
    low = (rest - mid.astype(F32)).astype(BF16)
    return hi, mid, low


def attend(q, held):
    m = jnp.full((ROWS, 1), NEG, F32)
    l = jnp.zeros((ROWS, 1), F32)
    acc = jnp.zeros((ROWS, HD), F32)
    for keys, values in held:
        for i in range(0, HALF, CHUNK):
            at = pl.ds(i, CHUNK)
            s = dot_t(q, keys[at])
            m_new = jnp.maximum(m, jnp.max(s, axis=-1, keepdims=True) * SCALE2)
            fade = jnp.exp2(m - m_new)
            w = jnp.exp2(s * SCALE2 - m_new)
            l = l * fade + jnp.sum(w, axis=-1, keepdims=True)
            acc = acc * fade + dot(w.astype(BF16), values[at])
            m = m_new
    return acc / l, m + jnp.log2(l)


def deal_kernel(x_ref, kept, came, *outs):
    for k, out in enumerate(outs):
        to = lax.rem(x_ref[0] + k, 4)
        out[0] = kept[to]
        out[1] = came[to]


def sort_kernel(*refs):
    *blocks, keys, rest = refs
    for n, (got, i) in enumerate((got, i) for got in blocks for i in range(2)):
        keys[pl.ds(n * BLOCK, BLOCK)] = got[i, pl.ds(0, BLOCK)]
        rest[pl.ds(n * BLOCK, BLOCK)] = got[i, pl.ds(BLOCK, BLOCK)]
        rest[pl.ds(HALF + n * SUF, SUF)] = got[i, pl.ds(2 * BLOCK, SUF)]


def on_diagonal(rows):
    row = lax.broadcasted_iota(jnp.int32, (rows, LANES), 0)
    return row == lax.broadcasted_iota(jnp.int32, (rows, LANES), 1)


def unit(u):
    return pl.ds(u * LANES, LANES)


def to_line(column):
    return jnp.sum(jnp.where(on_diagonal(column.shape[0]), column, 0.0), axis=0, keepdims=True)


def to_column(line, rows):
    return jnp.sum(jnp.where(on_diagonal(rows), line, 0.0), axis=1, keepdims=True)


def store_lines(out_ref, lines):
    lines = jnp.concatenate(lines + [jnp.zeros((8 - UNITS, LANES), F32)], axis=0)
    if out_ref.dtype == BF16:
        parts = [part.astype(F32) for part in split3(lines)]
        lines = jnp.concatenate(parts + [jnp.zeros((8, LANES), F32)], axis=0).astype(BF16)
    out_ref[pl.ds(ROWS, lines.shape[0])] = lines


def load_lines(ref):
    if ref.dtype == BF16:
        parts = ref[pl.ds(ROWS, PACKED - ROWS)].astype(F32)
        return parts[0:8] + parts[8:16] + parts[16:24]
    return ref[pl.ds(ROWS, PACKED_WIDE - ROWS)]


def pack(o, lse):
    line = to_line(lse)
    hi, mid, low = (jnp.broadcast_to(part.astype(F32), (EXTRA, HD)) for part in split3(line))
    row = lax.broadcasted_iota(jnp.int32, (EXTRA, HD), 0)
    parts = jnp.where(row == 0, hi, jnp.where(row == 1, mid, jnp.where(row == 2, low, 0.0)))
    return jnp.concatenate([o, parts], axis=0).astype(BF16)


def unpack(piece):
    piece = piece.astype(F32)
    line = jnp.sum(piece[PIECE:], axis=0, keepdims=True)
    return piece[:PIECE], to_column(line, PIECE)


def attend_kernel(q_ref, k_a, v_a, k_b, v_b, out_ref, lse_sc):
    o, lse = attend(q_ref[...], ((k_a, v_a), (k_b, v_b)))
    out_ref[pl.ds(0, ROWS)] = o.astype(out_ref.dtype)
    lse_sc[...] = jnp.broadcast_to(lse, (ROWS, LANES))
    store_lines(out_ref, [to_line(lse_sc[unit(u)]) for u in range(UNITS)])


def join(o1, lse1, o2, lse2):
    top = jnp.maximum(lse1, lse2)
    w1, w2 = jnp.exp2(lse1 - top), jnp.exp2(lse2 - top)
    total = w1 + w2
    return (w1 * o1 + w2 * o2) / total, top + jnp.log2(total)


def join_kernel(a_ref, b_ref, out_ref, o_sc, lse_sc):
    lines_a, lines_b = load_lines(a_ref), load_lines(b_ref)
    for u in range(UNITS):
        lse_a, lse_b = (to_column(lines[u : u + 1], LANES) for lines in (lines_a, lines_b))
        o, lse = join(a_ref[unit(u)].astype(F32), lse_a, b_ref[unit(u)].astype(F32), lse_b)
        o_sc[unit(u)] = o
        lse_sc[unit(u)] = jnp.broadcast_to(lse, (LANES, LANES))
    for p in range(PIECES):
        at = pl.ds(p * PIECE, PIECE)
        out_ref[p] = pack(o_sc[at], lse_sc[at])


def suffix_kernel(q_ref, k_ref, v_ref, step_ref, sample_ref, o_ref, lse_ref):
    row = lax.broadcasted_iota(jnp.int32, (TOKENS, TOKENS), 0)
    keep = (sample_ref[...] == row % SAMPLES) & (step_ref[...] <= row // SAMPLES)
    for j in range(HEADS):
        at = pl.ds(j * TOKENS, TOKENS)
        t = jnp.where(keep, dot_t(q_ref[at], k_ref[...]) * SCALE2, NEG)
        m = jnp.max(t, axis=-1, keepdims=True)
        w = jnp.where(keep, jnp.exp2(t - m), 0.0)
        l = jnp.sum(w, axis=-1, keepdims=True)
        o_ref[at] = dot(w.astype(BF16), v_ref[...]) / l
        lse_ref[at] = jnp.broadcast_to(m + jnp.log2(l), (TOKENS, HD))


def merge_kernel(r_ref, o_ref, lse_ref, live_ref, out_ref):
    per_head = PIECES // HEADS
    for p in range(PIECES):
        at = pl.ds(p * PIECE, PIECE)
        tok = pl.ds((p % per_head) * PIECE, PIECE)
        merged, _ = join(o_ref[at], lse_ref[at], *unpack(r_ref[p]))
        merged = jnp.where(live_ref[tok] > 0, merged, 0.0)
        out_ref[tok, pl.ds((p // per_head) * HD, HD)] = merged.astype(BF16)


def call(kernel, outs, args, scratch=(), flops=0, exps=0, scalars=0):
    moved = sum(math.prod(a.shape) * a.dtype.itemsize for a in (*args, *outs))
    smem = pl.BlockSpec(memory_space=pltpu.SMEM)
    many = len(outs) > 1
    return pl.pallas_call(
        kernel,
        out_shape=tuple(outs) if many else outs[0],
        in_specs=[smem] * scalars + [VMEM] * (len(args) - scalars),
        out_specs=(VMEM,) * len(outs) if many else VMEM,
        scratch_shapes=list(scratch),
        compiler_params=pltpu.CompilerParams(vmem_limit_bytes=40 * 2**20),
        cost_estimate=pl.CostEstimate(flops=flops, bytes_accessed=moved, transcendentals=exps),
    )(*args)


def sds(*shape, dtype=F32):
    return jax.ShapeDtypeStruct(shape, dtype)


def exchange(a):
    order = [(i + FIRST) % PIECES for i in range(PIECES)]
    return lax.all_to_all(a, "prompt", 0, 0, tiled=True, axis_index_groups=[order])


def in_order(index):
    return (jnp.roll(index, -FIRST) + PIECES - FIRST) % PIECES


def local(
    prompt_keys, prompt_values, queries, sample_step_keys, suffix_values, suffix_lengths, assignment
):
    tp = lax.axis_index("tp")
    x, z, core = tp // 8, (tp // 2) % 4, tp % 2
    keys, values = prompt_keys[0], prompt_values[0]

    def turn(zz):
        return (zz % 2) * 2 + zz // 2

    def permute(a, target):
        pairs = []
        for t in range(32):
            to_x, to_z, to_core = target(t // 8, (t // 2) % 4, t % 2)
            pairs.append((t, 8 * to_x + 2 * to_z + to_core))
        return lax.ppermute(a, "tp", pairs)

    def there_0(xx, zz, cc):
        return xx, turn(zz), cc

    def there_1(xx, zz, cc):
        return xx, turn(zz) ^ 2, cc

    def back_1(xx, zz, cc):
        return xx, turn(zz ^ 2), cc

    fresh = jnp.stack([sample_step_keys[0], suffix_values[0]])
    fresh = jnp.transpose(fresh, (3, 0, 1, 2, 4)).reshape(8, 4 * STEPS, HD)
    fresh = jnp.pad(fresh, ((0, 0), (0, SUF - 4 * STEPS), (0, 0)))

    def of_parity(which):
        parts = [
            lax.dynamic_index_in_dim(a.reshape(4, 2, -1, HD), which, 1, keepdims=False)
            for a in (keys, values, fresh)
        ]
        return jnp.concatenate(parts, axis=1)

    rows = jnp.transpose(queries[0].reshape(TOKENS, HEADS, HD), (1, 0, 2))
    pieces = rows.reshape(PIECES, PIECE, HD)
    spread = exchange(pieces)
    index = jnp.arange(PIECES, dtype=jnp.int32)
    server = jnp.sum(jnp.where(assignment[None, :] == index[:, None], index[None, :], 0), axis=1)
    sorted_in = jnp.take(spread, in_order(server), axis=0, mode="clip")
    kept = of_parity(z % 2)
    came = permute(of_parity(1 - z % 2), lambda xx, zz, cc: (xx, zz ^ 1, cc))

    dealt = call(
        deal_kernel,
        [sds(2, PART, HD, dtype=BF16)] * 4,
        [x.reshape(1), kept, came],
        flops=SORT_FLOPS,
        scalars=1,
    )
    got = [dealt[0]]
    for k in (1, 2, 3):
        shift = lambda xx, zz, cc, k=k: ((xx + k) % 4, zz, cc)
        got.append(permute(dealt[k], shift))
    mine = call(
        sort_kernel,
        [sds(HALF, HD, dtype=BF16), sds(HALF + 8 * SUF, HD, dtype=BF16)],
        got,
        flops=SORT_FLOPS,
    )
    home = exchange(sorted_in).reshape(ROWS, HD)
    far = [permute(a, lambda xx, zz, cc: (xx, zz, cc ^ 1)) for a in mine]

    def cost(positions):
        return dict(flops=4 * ROWS * positions * HD, exps=ROWS * positions)

    held = [*mine, *far]
    wide = pltpu.VMEM((ROWS, HD), F32)
    partial = []
    for there, back, kind, size in (
        (there_0, there_0, BF16, PACKED),
        (there_1, back_1, F32, PACKED_WIDE),
    ):
        part = call(
            attend_kernel,
            [sds(size, HD, dtype=kind)],
            [permute(home, there), *held],
            scratch=[wide],
            **cost(4096),
        )
        partial.append(permute(part, back))
    done = call(
        join_kernel, [sds(PIECES, PIECE + EXTRA, HD, dtype=BF16)], partial, scratch=[wide, wide]
    )

    tail = jnp.stack([e[1][HALF:].reshape(8, SUF, HD) for e in (mine, far)])
    done, tail = lax.optimization_barrier((done, tail))
    tail = jnp.stack([permute(tail, there_0), permute(tail, back_1)])
    live = jnp.arange(STEPS, dtype=jnp.int32)[:, None] < suffix_lengths[0][None, :]
    live = jnp.broadcast_to(live.reshape(TOKENS, 1), (TOKENS, HD)).astype(jnp.int32)

    gone = exchange(done)
    gone, tail = lax.optimization_barrier((gone, tail))
    sorted_out = jnp.take(gone, in_order(assignment), axis=0, mode="clip")
    sorted_out, tail = lax.optimization_barrier((sorted_out, tail))
    suf_k = tail[:, :, :, : 2 * STEPS].reshape(TOKENS, HD)
    suf_v = tail[:, :, :, 2 * STEPS : 4 * STEPS].reshape(TOKENS, HD)
    shape = (2, 2, 4, 2, STEPS, 2)
    at = [lax.broadcasted_iota(jnp.int32, shape, d) for d in range(6)]
    origin = turn(z) ^ (2 * at[0])
    source = 8 * ((x - at[2]) % 4) + 2 * (origin ^ at[3]) + (core ^ at[1])
    sample, step = 2 * source + at[5], at[4]
    wide = (TOKENS, TOKENS)
    o_s, lse_s = call(
        suffix_kernel,
        [sds(ROWS, HD)] * 2,
        [
            rows.reshape(ROWS, HD),
            suf_k,
            suf_v,
            jnp.broadcast_to(step.reshape(1, TOKENS), wide),
            jnp.broadcast_to(sample.reshape(1, TOKENS), wide),
        ],
        flops=4 * ROWS * TOKENS * HD,
        exps=ROWS * TOKENS,
    )
    back = exchange(sorted_out)
    out = call(
        merge_kernel, [sds(TOKENS, HEADS * HD, dtype=BF16)], [back, o_s, lse_s, live]
    )
    return out.reshape(1, STEPS, SAMPLES, HEADS * HD)


def solution(mesh):
    in_specs = (
        P("prompt", None, "tp", None),
        P("prompt", None, "tp", None),
        P("prompt", None, None, "tp"),
        P("prompt", None, "tp", None, None),
        P("prompt", None, "tp", None, None),
        P("prompt", None),
        P(),
    )
    out_specs = P("prompt", None, None, "tp")
    return jax.shard_map(local, mesh=mesh, in_specs=in_specs, out_specs=out_specs, check_vma=False)
```

```python
import functools
import math

import jax
import jax.numpy as jnp
from jax import lax
from jax.experimental import pallas as pl
from jax.experimental.pallas import tpu as pltpu
from jax.sharding import PartitionSpec as P

F32 = jnp.float32
BF16 = jnp.bfloat16
NEG = -1e30
VMEM = pl.BlockSpec(memory_space=pltpu.VMEM)

STEPS, SAMPLES, HD = 3, 64, 128
HEADS = 4
TOKENS = STEPS * SAMPLES
ROWS = HEADS * TOKENS
BLOCK = 256
SUF = 16
PART = 2 * BLOCK + SUF
HALF = 8 * BLOCK
SORT_FLOPS = 40 * 10**9
PIECES = 16
PIECE = ROWS // PIECES
EXTRA = 8
LANES = 128
UNITS = ROWS // LANES
PACKED = ROWS + 32
PACKED_WIDE = ROWS + 8
SCALE2 = HD ** (-0.5) * math.log2(math.e)
CHUNK = 1024
FIRST = 10


def dot_t(a, b):
    return lax.dot_general(a, b, (((1,), (1,)), ((), ())), preferred_element_type=F32)


def dot(a, b):
    return lax.dot_general(a, b, (((1,), (0,)), ((), ())), preferred_element_type=F32)


def split3(x):
    hi = x.astype(BF16)
    rest = x - hi.astype(F32)
    mid = rest.astype(BF16)
    low = (rest - mid.astype(F32)).astype(BF16)
    return hi, mid, low


def attend(q, held):
    m = jnp.full((ROWS, 1), NEG, F32)
    l = jnp.zeros((ROWS, 1), F32)
    acc = jnp.zeros((ROWS, HD), F32)
    for keys, values in held:
        for i in range(0, HALF, CHUNK):
            at = pl.ds(i, CHUNK)
            s = dot_t(q, keys[at])
            m_new = jnp.maximum(m, jnp.max(s, axis=-1, keepdims=True) * SCALE2)
            fade = jnp.exp2(m - m_new)
            w = jnp.exp2(s * SCALE2 - m_new)
            l = l * fade + jnp.sum(w, axis=-1, keepdims=True)
            acc = acc * fade + dot(w.astype(BF16), values[at])
            m = m_new
    return acc / l, m + jnp.log2(l)


def deal_kernel(x_ref, kept, came, *outs):
    for k, out in enumerate(outs):
        to = lax.rem(x_ref[0] + k, 4)
        out[0] = kept[to]
        out[1] = came[to]


def sort_kernel(*refs):
    *blocks, keys, rest = refs
    for n, (got, i) in enumerate((got, i) for got in blocks for i in range(2)):
        keys[pl.ds(n * BLOCK, BLOCK)] = got[i, pl.ds(0, BLOCK)]
        rest[pl.ds(n * BLOCK, BLOCK)] = got[i, pl.ds(BLOCK, BLOCK)]
        rest[pl.ds(HALF + n * SUF, SUF)] = got[i, pl.ds(2 * BLOCK, SUF)]


def on_diagonal(rows):
    row = lax.broadcasted_iota(jnp.int32, (rows, LANES), 0)
    return row == lax.broadcasted_iota(jnp.int32, (rows, LANES), 1)


def unit(u):
    return pl.ds(u * LANES, LANES)


def to_line(column):
    return jnp.sum(jnp.where(on_diagonal(column.shape[0]), column, 0.0), axis=0, keepdims=True)


def to_column(line, rows):
    return jnp.sum(jnp.where(on_diagonal(rows), line, 0.0), axis=1, keepdims=True)


def store_lines(out_ref, lines):
    lines = jnp.concatenate(lines + [jnp.zeros((8 - UNITS, LANES), F32)], axis=0)
    if out_ref.dtype == BF16:
        parts = [part.astype(F32) for part in split3(lines)]
        lines = jnp.concatenate(parts + [jnp.zeros((8, LANES), F32)], axis=0).astype(BF16)
    out_ref[pl.ds(ROWS, lines.shape[0])] = lines


def load_lines(ref):
    if ref.dtype == BF16:
        parts = ref[pl.ds(ROWS, PACKED - ROWS)].astype(F32)
        return parts[0:8] + parts[8:16] + parts[16:24]
    return ref[pl.ds(ROWS, PACKED_WIDE - ROWS)]


def pack(o, lse):
    line = to_line(lse)
    hi, mid, low = (jnp.broadcast_to(part.astype(F32), (EXTRA, HD)) for part in split3(line))
    row = lax.broadcasted_iota(jnp.int32, (EXTRA, HD), 0)
    parts = jnp.where(row == 0, hi, jnp.where(row == 1, mid, jnp.where(row == 2, low, 0.0)))
    return jnp.concatenate([o, parts], axis=0).astype(BF16)


def unpack(piece):
    piece = piece.astype(F32)
    line = jnp.sum(piece[PIECE:], axis=0, keepdims=True)
    return piece[:PIECE], to_column(line, PIECE)


def attend_kernel(q_ref, k_a, v_a, k_b, v_b, out_ref, lse_sc):
    o, lse = attend(q_ref[...], ((k_a, v_a), (k_b, v_b)))
    out_ref[pl.ds(0, ROWS)] = o.astype(out_ref.dtype)
    lse_sc[...] = jnp.broadcast_to(lse, (ROWS, LANES))
    store_lines(out_ref, [to_line(lse_sc[unit(u)]) for u in range(UNITS)])
    if out_ref.shape[0] > PACKED:
        for n, v in enumerate((v_a, v_b)):
            out_ref[pl.ds(PACKED + n * 8 * SUF, 8 * SUF)] = v[pl.ds(HALF, 8 * SUF)]


def join(o1, lse1, o2, lse2):
    top = jnp.maximum(lse1, lse2)
    w1, w2 = jnp.exp2(lse1 - top), jnp.exp2(lse2 - top)
    total = w1 + w2
    return (w1 * o1 + w2 * o2) / total, top + jnp.log2(total)


def join_kernel(a_ref, b_ref, out_ref, o_sc, lse_sc):
    lines_a, lines_b = load_lines(a_ref), load_lines(b_ref)
    for u in range(UNITS):
        lse_a, lse_b = (to_column(lines[u : u + 1], LANES) for lines in (lines_a, lines_b))
        o, lse = join(a_ref[unit(u)].astype(F32), lse_a, b_ref[unit(u)].astype(F32), lse_b)
        o_sc[unit(u)] = o
        lse_sc[unit(u)] = jnp.broadcast_to(lse, (LANES, LANES))
    for p in range(PIECES):
        at = pl.ds(p * PIECE, PIECE)
        out_ref[p] = pack(o_sc[at], lse_sc[at])


def suffix_kernel(q_ref, k_ref, v_ref, step_ref, sample_ref, o_ref, lse_ref):
    row = lax.broadcasted_iota(jnp.int32, (TOKENS, TOKENS), 0)
    keep = (sample_ref[...] == row % SAMPLES) & (step_ref[...] <= row // SAMPLES)
    for j in range(HEADS):
        at = pl.ds(j * TOKENS, TOKENS)
        t = jnp.where(keep, dot_t(q_ref[at], k_ref[...]) * SCALE2, NEG)
        m = jnp.max(t, axis=-1, keepdims=True)
        w = jnp.where(keep, jnp.exp2(t - m), 0.0)
        l = jnp.sum(w, axis=-1, keepdims=True)
        o_ref[at] = dot(w.astype(BF16), v_ref[...]) / l
        lse_ref[at] = jnp.broadcast_to(m + jnp.log2(l), (TOKENS, HD))


def merge_kernel(r_ref, o_ref, lse_ref, live_ref, out_ref):
    per_head = PIECES // HEADS
    for p in range(PIECES):
        at = pl.ds(p * PIECE, PIECE)
        tok = pl.ds((p % per_head) * PIECE, PIECE)
        merged, _ = join(o_ref[at], lse_ref[at], *unpack(r_ref[p]))
        merged = jnp.where(live_ref[tok] > 0, merged, 0.0)
        out_ref[tok, pl.ds((p // per_head) * HD, HD)] = merged.astype(BF16)


def call(kernel, outs, args, scratch=(), flops=0, exps=0, scalars=0):
    moved = sum(math.prod(a.shape) * a.dtype.itemsize for a in (*args, *outs))
    smem = pl.BlockSpec(memory_space=pltpu.SMEM)
    many = len(outs) > 1
    return pl.pallas_call(
        kernel,
        out_shape=tuple(outs) if many else outs[0],
        in_specs=[smem] * scalars + [VMEM] * (len(args) - scalars),
        out_specs=(VMEM,) * len(outs) if many else VMEM,
        scratch_shapes=list(scratch),
        compiler_params=pltpu.CompilerParams(vmem_limit_bytes=40 * 2**20),
        cost_estimate=pl.CostEstimate(flops=flops, bytes_accessed=moved, transcendentals=exps),
    )(*args)


def sds(*shape, dtype=F32):
    return jax.ShapeDtypeStruct(shape, dtype)


def exchange(a):
    order = [(i + FIRST) % PIECES for i in range(PIECES)]
    return lax.all_to_all(a, "prompt", 0, 0, tiled=True, axis_index_groups=[order])


def in_order(index):
    return (jnp.roll(index, -FIRST) + PIECES - FIRST) % PIECES


def local(
    prompt_keys, prompt_values, queries, sample_step_keys, suffix_values, suffix_lengths, assignment
):
    tp = lax.axis_index("tp")
    x, z, core = tp // 8, (tp // 2) % 4, tp % 2
    keys, values = prompt_keys[0], prompt_values[0]

    def turn(zz):
        return (zz % 2) * 2 + zz // 2

    def permute(a, target):
        pairs = []
        for t in range(32):
            to_x, to_z, to_core = target(t // 8, (t // 2) % 4, t % 2)
            pairs.append((t, 8 * to_x + 2 * to_z + to_core))
        return lax.ppermute(a, "tp", pairs)

    def there_0(xx, zz, cc):
        return xx, turn(zz), cc

    def there_1(xx, zz, cc):
        return xx, turn(zz) ^ 2, cc

    def back_1(xx, zz, cc):
        return xx, turn(zz ^ 2), cc

    fresh = jnp.stack([sample_step_keys[0], suffix_values[0]])
    fresh = jnp.transpose(fresh, (3, 0, 1, 2, 4)).reshape(8, 4 * STEPS, HD)
    fresh = jnp.pad(fresh, ((0, 0), (0, SUF - 4 * STEPS), (0, 0)))

    def of_parity(which):
        parts = [
            lax.dynamic_index_in_dim(a.reshape(4, 2, -1, HD), which, 1, keepdims=False)
            for a in (keys, values, fresh)
        ]
        return jnp.concatenate(parts, axis=1)

    rows = jnp.transpose(queries[0].reshape(TOKENS, HEADS, HD), (1, 0, 2))
    pieces = rows.reshape(PIECES, PIECE, HD)
    spread = exchange(pieces)
    index = jnp.arange(PIECES, dtype=jnp.int32)
    server = jnp.sum(jnp.where(assignment[None, :] == index[:, None], index[None, :], 0), axis=1)
    sorted_in = jnp.take(spread, in_order(server), axis=0, mode="clip")
    kept = of_parity(z % 2)
    came = permute(of_parity(1 - z % 2), lambda xx, zz, cc: (xx, zz ^ 1, cc))

    dealt = call(
        deal_kernel,
        [sds(2, PART, HD, dtype=BF16)] * 4,
        [x.reshape(1), kept, came],
        flops=SORT_FLOPS,
        scalars=1,
    )
    got = [dealt[0]]
    for k in (1, 2, 3):
        shift = lambda xx, zz, cc, k=k: ((xx + k) % 4, zz, cc)
        got.append(permute(dealt[k], shift))
    mine = call(
        sort_kernel,
        [sds(HALF, HD, dtype=BF16), sds(HALF + 8 * SUF, HD, dtype=BF16)],
        got,
        flops=SORT_FLOPS,
    )
    home = exchange(sorted_in).reshape(ROWS, HD)
    far = [permute(a, lambda xx, zz, cc: (xx, zz, cc ^ 1)) for a in mine]

    def cost(positions):
        return dict(flops=4 * ROWS * positions * HD, exps=ROWS * positions)

    held = [*mine, *far]
    wide = pltpu.VMEM((ROWS, HD), F32)
    partial = []
    for there, back, kind, size in (
        (there_1, back_1, BF16, PACKED + 16 * SUF),
        (there_0, there_0, BF16, PACKED),
    ):
        part = call(
            attend_kernel,
            [sds(size, HD, dtype=kind)],
            [permute(home, there), *held],
            scratch=[wide],
            **cost(4096),
        )
        partial.append(permute(part, back))
    done = call(
        join_kernel, [sds(PIECES, PIECE + EXTRA, HD, dtype=BF16)], partial, scratch=[wide, wide]
    )

    tail = jnp.stack([e[1][HALF:].reshape(8, SUF, HD) for e in (mine, far)])
    done, tail = lax.optimization_barrier((done, tail))
    tail = jnp.stack([permute(tail, there_0), partial[0][PACKED:].reshape(tail.shape)])
    live = jnp.arange(STEPS, dtype=jnp.int32)[:, None] < suffix_lengths[0][None, :]
    live = jnp.broadcast_to(live.reshape(TOKENS, 1), (TOKENS, HD)).astype(jnp.int32)

    gone = exchange(done)
    gone, tail = lax.optimization_barrier((gone, tail))
    sorted_out = jnp.take(gone, in_order(assignment), axis=0, mode="clip")
    sorted_out, tail = lax.optimization_barrier((sorted_out, tail))
    suf_k = tail[:, :, :, : 2 * STEPS].reshape(TOKENS, HD)
    suf_v = tail[:, :, :, 2 * STEPS : 4 * STEPS].reshape(TOKENS, HD)
    shape = (2, 2, 4, 2, STEPS, 2)
    at = [lax.broadcasted_iota(jnp.int32, shape, d) for d in range(6)]
    origin = turn(z) ^ (2 * at[0])
    source = 8 * ((x - at[2]) % 4) + 2 * (origin ^ at[3]) + (core ^ at[1])
    sample, step = 2 * source + at[5], at[4]
    wide = (TOKENS, TOKENS)
    o_s, lse_s = call(
        suffix_kernel,
        [sds(ROWS, HD)] * 2,
        [
            rows.reshape(ROWS, HD),
            suf_k,
            suf_v,
            jnp.broadcast_to(step.reshape(1, TOKENS), wide),
            jnp.broadcast_to(sample.reshape(1, TOKENS), wide),
        ],
        flops=4 * ROWS * TOKENS * HD,
        exps=ROWS * TOKENS,
    )
    back = exchange(sorted_out)
    out = call(
        merge_kernel, [sds(TOKENS, HEADS * HD, dtype=BF16)], [back, o_s, lse_s, live]
    )
    return out.reshape(1, STEPS, SAMPLES, HEADS * HD)


def solution(mesh):
    in_specs = (
        P("prompt", None, "tp", None),
        P("prompt", None, "tp", None),
        P("prompt", None, None, "tp"),
        P("prompt", None, "tp", None, None),
        P("prompt", None, "tp", None, None),
        P("prompt", None),
        P(),
    )
    out_specs = P("prompt", None, None, "tp")
    return jax.shard_map(local, mesh=mesh, in_specs=in_specs, out_specs=out_specs, check_vma=False)
```

```python
import functools
import math

import jax
import jax.numpy as jnp
from jax import lax
from jax.experimental import pallas as pl
from jax.experimental.pallas import tpu as pltpu
from jax.sharding import PartitionSpec as P

F32 = jnp.float32
BF16 = jnp.bfloat16
NEG = -1e30
VMEM = pl.BlockSpec(memory_space=pltpu.VMEM)

STEPS, SAMPLES, HD = 3, 64, 128
HEADS = 4
TOKENS = STEPS * SAMPLES
ROWS = HEADS * TOKENS
BLOCK = 256
SUF = 16
PART = 2 * BLOCK + SUF
HALF = 8 * BLOCK
SORT_FLOPS = 40 * 10**9
PIECES = 16
PIECE = ROWS // PIECES
EXTRA = 8
LANES = 128
UNITS = ROWS // LANES
PACKED = ROWS + 32
PACKED_WIDE = ROWS + 8
SCALE2 = HD ** (-0.5) * math.log2(math.e)
CHUNK = 1024
FIRST = 10


def dot_t(a, b):
    return lax.dot_general(a, b, (((1,), (1,)), ((), ())), preferred_element_type=F32)


def dot(a, b):
    return lax.dot_general(a, b, (((1,), (0,)), ((), ())), preferred_element_type=F32)


def split3(x):
    hi = x.astype(BF16)
    rest = x - hi.astype(F32)
    mid = rest.astype(BF16)
    low = (rest - mid.astype(F32)).astype(BF16)
    return hi, mid, low


def attend(q, held):
    m = jnp.full((ROWS, 1), NEG, F32)
    l = jnp.zeros((ROWS, 1), F32)
    acc = jnp.zeros((ROWS, HD), F32)
    for keys, values in held:
        for i in range(0, HALF, CHUNK):
            at = pl.ds(i, CHUNK)
            s = dot_t(q, keys[at])
            m_new = jnp.maximum(m, jnp.max(s, axis=-1, keepdims=True) * SCALE2)
            fade = jnp.exp2(m - m_new)
            w = jnp.exp2(s * SCALE2 - m_new)
            l = l * fade + jnp.sum(w, axis=-1, keepdims=True)
            acc = acc * fade + dot(w.astype(BF16), values[at])
            m = m_new
    return acc / l, m + jnp.log2(l)


def deal_kernel(x_ref, kept, came, *outs):
    for k, out in enumerate(outs):
        to = lax.rem(x_ref[0] + k, 4)
        out[0] = kept[to]
        out[1] = came[to]


def sort_kernel(*refs):
    *blocks, keys, rest = refs
    for n, (got, i) in enumerate((got, i) for got in blocks for i in range(2)):
        keys[pl.ds(n * BLOCK, BLOCK)] = got[i, pl.ds(0, BLOCK)]
        rest[pl.ds(n * BLOCK, BLOCK)] = got[i, pl.ds(BLOCK, BLOCK)]
        rest[pl.ds(HALF + n * SUF, SUF)] = got[i, pl.ds(2 * BLOCK, SUF)]


def on_diagonal(rows):
    row = lax.broadcasted_iota(jnp.int32, (rows, LANES), 0)
    return row == lax.broadcasted_iota(jnp.int32, (rows, LANES), 1)


def unit(u):
    return pl.ds(u * LANES, LANES)


def to_line(column):
    return jnp.sum(jnp.where(on_diagonal(column.shape[0]), column, 0.0), axis=0, keepdims=True)


def to_column(line, rows):
    return jnp.sum(jnp.where(on_diagonal(rows), line, 0.0), axis=1, keepdims=True)


def store_lines(out_ref, lines):
    lines = jnp.concatenate(lines + [jnp.zeros((8 - UNITS, LANES), F32)], axis=0)
    if out_ref.dtype == BF16:
        parts = [part.astype(F32) for part in split3(lines)]
        lines = jnp.concatenate(parts + [jnp.zeros((8, LANES), F32)], axis=0).astype(BF16)
    out_ref[pl.ds(ROWS, lines.shape[0])] = lines


def load_lines(ref):
    if ref.dtype == BF16:
        parts = ref[pl.ds(ROWS, PACKED - ROWS)].astype(F32)
        return parts[0:8] + parts[8:16] + parts[16:24]
    return ref[pl.ds(ROWS, PACKED_WIDE - ROWS)]


def pack(o, lse):
    line = to_line(lse)
    hi, mid, low = (jnp.broadcast_to(part.astype(F32), (EXTRA, HD)) for part in split3(line))
    row = lax.broadcasted_iota(jnp.int32, (EXTRA, HD), 0)
    parts = jnp.where(row == 0, hi, jnp.where(row == 1, mid, jnp.where(row == 2, low, 0.0)))
    return jnp.concatenate([o, parts], axis=0).astype(BF16)


def unpack(piece):
    piece = piece.astype(F32)
    line = jnp.sum(piece[PIECE:], axis=0, keepdims=True)
    return piece[:PIECE], to_column(line, PIECE)


def attend_kernel(q_ref, k_a, v_a, k_b, v_b, out_ref, lse_sc):
    o, lse = attend(q_ref[...], ((k_a, v_a), (k_b, v_b)))
    out_ref[pl.ds(0, ROWS)] = o.astype(out_ref.dtype)
    lse_sc[...] = jnp.broadcast_to(lse, (ROWS, LANES))
    store_lines(out_ref, [to_line(lse_sc[unit(u)]) for u in range(UNITS)])
    if out_ref.shape[0] > PACKED:
        for n, v in enumerate((v_a, v_b)):
            out_ref[pl.ds(PACKED + n * 8 * SUF, 8 * SUF)] = v[pl.ds(HALF, 8 * SUF)]


def join(o1, lse1, o2, lse2):
    top = jnp.maximum(lse1, lse2)
    w1, w2 = jnp.exp2(lse1 - top), jnp.exp2(lse2 - top)
    total = w1 + w2
    return (w1 * o1 + w2 * o2) / total, top + jnp.log2(total)


def join_kernel(a_ref, b_ref, out_ref, o_sc, lse_sc):
    lines_a, lines_b = load_lines(a_ref), load_lines(b_ref)
    for u in range(UNITS):
        lse_a, lse_b = (to_column(lines[u : u + 1], LANES) for lines in (lines_a, lines_b))
        o, lse = join(a_ref[unit(u)].astype(F32), lse_a, b_ref[unit(u)].astype(F32), lse_b)
        o_sc[unit(u)] = o
        lse_sc[unit(u)] = jnp.broadcast_to(lse, (LANES, LANES))
    for p in range(PIECES):
        at = pl.ds(p * PIECE, PIECE)
        out_ref[p] = pack(o_sc[at], lse_sc[at])


def suffix_kernel(q_ref, k_ref, v_ref, step_ref, sample_ref, o_ref, lse_ref):
    row = lax.broadcasted_iota(jnp.int32, (TOKENS, TOKENS), 0)
    keep = (sample_ref[...] == row % SAMPLES) & (step_ref[...] <= row // SAMPLES)
    for j in range(HEADS):
        at = pl.ds(j * TOKENS, TOKENS)
        t = jnp.where(keep, dot_t(q_ref[at], k_ref[...]) * SCALE2, NEG)
        m = jnp.max(t, axis=-1, keepdims=True)
        w = jnp.where(keep, jnp.exp2(t - m), 0.0)
        l = jnp.sum(w, axis=-1, keepdims=True)
        o_ref[at] = dot(w.astype(BF16), v_ref[...]) / l
        lse_ref[at] = jnp.broadcast_to(m + jnp.log2(l), (TOKENS, HD))


def merge_kernel(r_ref, o_ref, lse_ref, live_ref, out_ref):
    per_head = PIECES // HEADS
    for p in range(PIECES):
        at = pl.ds(p * PIECE, PIECE)
        tok = pl.ds((p % per_head) * PIECE, PIECE)
        merged, _ = join(o_ref[at], lse_ref[at], *unpack(r_ref[p]))
        merged = jnp.where(live_ref[tok] > 0, merged, 0.0)
        out_ref[tok, pl.ds((p // per_head) * HD, HD)] = merged.astype(BF16)


def call(kernel, outs, args, scratch=(), flops=0, exps=0, scalars=0):
    moved = sum(math.prod(a.shape) * a.dtype.itemsize for a in (*args, *outs))
    smem = pl.BlockSpec(memory_space=pltpu.SMEM)
    many = len(outs) > 1
    return pl.pallas_call(
        kernel,
        out_shape=tuple(outs) if many else outs[0],
        in_specs=[smem] * scalars + [VMEM] * (len(args) - scalars),
        out_specs=(VMEM,) * len(outs) if many else VMEM,
        scratch_shapes=list(scratch),
        compiler_params=pltpu.CompilerParams(vmem_limit_bytes=40 * 2**20),
        cost_estimate=pl.CostEstimate(flops=flops, bytes_accessed=moved, transcendentals=exps),
    )(*args)


def sds(*shape, dtype=F32):
    return jax.ShapeDtypeStruct(shape, dtype)


def exchange(a):
    order = [(i + FIRST) % PIECES for i in range(PIECES)]
    return lax.all_to_all(a, "prompt", 0, 0, tiled=True, axis_index_groups=[order])


def in_order(index):
    return (jnp.roll(index, -FIRST) + PIECES - FIRST) % PIECES


def local(
    prompt_keys, prompt_values, queries, sample_step_keys, suffix_values, suffix_lengths, assignment
):
    tp = lax.axis_index("tp")
    x, z, core = tp // 8, (tp // 2) % 4, tp % 2
    keys, values = prompt_keys[0], prompt_values[0]

    def turn(zz):
        return (zz % 2) * 2 + zz // 2

    def permute(a, target):
        pairs = []
        for t in range(32):
            to_x, to_z, to_core = target(t // 8, (t // 2) % 4, t % 2)
            pairs.append((t, 8 * to_x + 2 * to_z + to_core))
        return lax.ppermute(a, "tp", pairs)

    def there_0(xx, zz, cc):
        return xx, turn(zz), cc

    def there_1(xx, zz, cc):
        return xx, turn(zz) ^ 2, cc

    def back_1(xx, zz, cc):
        return xx, turn(zz ^ 2), cc

    fresh = jnp.stack([sample_step_keys[0], suffix_values[0]]).reshape(4 * STEPS, 4, 2, HD)

    def of_parity(which):
        parts = [
            lax.dynamic_index_in_dim(a.reshape(4, 2, -1, HD), which, 1, keepdims=False)
            for a in (keys, values)
        ]
        tokens = jnp.where(which == 0, fresh[:, :, 0], fresh[:, :, 1])
        tokens = jnp.pad(jnp.transpose(tokens, (1, 0, 2)), ((0, 0), (0, SUF - 4 * STEPS), (0, 0)))
        return jnp.concatenate([*parts, tokens], axis=1)

    rows = jnp.transpose(queries[0].reshape(TOKENS, HEADS, HD), (1, 0, 2))
    pieces = rows.reshape(PIECES, PIECE, HD)
    spread = exchange(pieces)
    index = jnp.arange(PIECES, dtype=jnp.int32)
    server = jnp.sum(jnp.where(assignment[None, :] == index[:, None], index[None, :], 0), axis=1)
    sorted_in = jnp.take(spread, in_order(server), axis=0, mode="clip")
    kept = of_parity(z % 2)
    came = permute(of_parity(1 - z % 2), lambda xx, zz, cc: (xx, zz ^ 1, cc))

    dealt = call(
        deal_kernel,
        [sds(2, PART, HD, dtype=BF16)] * 4,
        [x.reshape(1), kept, came],
        flops=SORT_FLOPS,
        scalars=1,
    )
    got = [dealt[0]]
    for k in (1, 2, 3):
        shift = lambda xx, zz, cc, k=k: ((xx + k) % 4, zz, cc)
        got.append(permute(dealt[k], shift))
    mine = call(
        sort_kernel,
        [sds(HALF, HD, dtype=BF16), sds(HALF + 8 * SUF, HD, dtype=BF16)],
        got,
        flops=SORT_FLOPS,
    )
    home = exchange(sorted_in).reshape(ROWS, HD)
    far = [permute(a, lambda xx, zz, cc: (xx, zz, cc ^ 1)) for a in mine]

    def cost(positions):
        return dict(flops=4 * ROWS * positions * HD, exps=ROWS * positions)

    held = [*mine, *far]
    wide = pltpu.VMEM((ROWS, HD), F32)
    partial = []
    for there, back, kind, size in (
        (there_1, back_1, BF16, PACKED + 16 * SUF),
        (there_0, there_0, BF16, PACKED),
    ):
        part = call(
            attend_kernel,
            [sds(size, HD, dtype=kind)],
            [permute(home, there), *held],
            scratch=[wide],
            **cost(4096),
        )
        partial.append(permute(part, back))
    done = call(
        join_kernel, [sds(PIECES, PIECE + EXTRA, HD, dtype=BF16)], partial, scratch=[wide, wide]
    )

    tail = jnp.stack([e[1][HALF:].reshape(8, SUF, HD) for e in (mine, far)])
    done, tail = lax.optimization_barrier((done, tail))
    tail = jnp.stack([permute(tail, there_0), partial[0][PACKED:].reshape(tail.shape)])
    live = jnp.arange(STEPS, dtype=jnp.int32)[:, None] < suffix_lengths[0][None, :]
    live = jnp.broadcast_to(live.reshape(TOKENS, 1), (TOKENS, HD)).astype(jnp.int32)

    gone = exchange(done)
    gone, tail = lax.optimization_barrier((gone, tail))
    sorted_out = jnp.take(gone, in_order(assignment), axis=0, mode="clip")
    sorted_out, tail = lax.optimization_barrier((sorted_out, tail))
    suf_k = tail[:, :, :, : 2 * STEPS].reshape(TOKENS, HD)
    suf_v = tail[:, :, :, 2 * STEPS : 4 * STEPS].reshape(TOKENS, HD)
    shape = (2, 2, 4, 2, STEPS, 2)
    at = [lax.broadcasted_iota(jnp.int32, shape, d) for d in range(6)]
    origin = turn(z) ^ (2 * at[0])
    source = 8 * ((x - at[2]) % 4) + 2 * (origin ^ at[3]) + (core ^ at[1])
    sample, step = 2 * source + at[5], at[4]
    wide = (TOKENS, TOKENS)
    o_s, lse_s = call(
        suffix_kernel,
        [sds(ROWS, HD)] * 2,
        [
            rows.reshape(ROWS, HD),
            suf_k,
            suf_v,
            jnp.broadcast_to(step.reshape(1, TOKENS), wide),
            jnp.broadcast_to(sample.reshape(1, TOKENS), wide),
        ],
        flops=4 * ROWS * TOKENS * HD,
        exps=ROWS * TOKENS,
    )
    back = exchange(sorted_out)
    out = call(
        merge_kernel, [sds(TOKENS, HEADS * HD, dtype=BF16)], [back, o_s, lse_s, live]
    )
    return out.reshape(1, STEPS, SAMPLES, HEADS * HD)


def solution(mesh):
    in_specs = (
        P("prompt", None, "tp", None),
        P("prompt", None, "tp", None),
        P("prompt", None, None, "tp"),
        P("prompt", None, "tp", None, None),
        P("prompt", None, "tp", None, None),
        P("prompt", None),
        P(),
    )
    out_specs = P("prompt", None, None, "tp")
    return jax.shard_map(local, mesh=mesh, in_specs=in_specs, out_specs=out_specs, check_vma=False)
```
